128 devices in a mesh: expert: 32 (over z, x, core), fsdp: 4 (over y).
Axes of the slice: x: 4, y: 4, z: 4, core: 2. Of those that a mesh axis runs over, the one named last changes fastest.
Arguments:
- hidden: bfloat16 [24576, 1024], P(('expert', 'fsdp')), may hold values from -6 to 6
- segments: int32 [24576], P(('expert', 'fsdp')), may hold values from 0 to 2, as said below
- routes: int32 [24576, 8], P(('expert', 'fsdp')), may hold values from 0 to 31, all different within a row; in each aligned block of 192 rows (0 to 191, 192 to 383, ...) at most 72 rows name the same one
- attention_gain: bfloat16 [1024], P('fsdp'), may hold values from 0.25 to 1.75
- query_weight: bfloat16 [1024, 1024], P('fsdp'), may hold values from -0.1875 to 0.1875
- key_weight: bfloat16 [1024, 512], P('fsdp'), may hold values from -0.1875 to 0.1875
- value_weight: bfloat16 [1024, 512], P('fsdp'), may hold values from -0.1875 to 0.1875
- projection_weight: bfloat16 [1024, 1024], P('fsdp'), may hold values from -1 to 1
- mixture_gain: bfloat16 [1024], P('fsdp'), may hold values from 0.25 to 1.75
- router_weight: bfloat16 [1024, 32], P('fsdp'), may hold values from -0.09375 to 0.09375
- gate_weight: bfloat16 [32, 1024, 512], P('expert', 'fsdp'), may hold values from -0.1875 to 0.1875
- up_weight: bfloat16 [32, 1024, 512], P('expert', 'fsdp'), may hold values from -0.1875 to 0.1875
- down_weight: bfloat16 [32, 512, 1024], P('expert', 'fsdp'), may hold values from -1 to 1
- cotangent: bfloat16 [24576, 1024], P(('expert', 'fsdp')), may hold values from -6 to 6
Outputs:
- output: bfloat16 [24576, 1024], P(('expert', 'fsdp'))
- input_gradient: float32 [24576, 1024], P(('expert', 'fsdp'))
- attention_gain_gradient: float32 [1024], P('fsdp')
- query_gradient: float32 [1024, 1024], P('fsdp')
- key_gradient: float32 [1024, 512], P('fsdp')
- value_gradient: float32 [1024, 512], P('fsdp')
- projection_gradient: float32 [1024, 1024], P('fsdp')
- mixture_gain_gradient: float32 [1024], P('fsdp')
- router_gradient: float32 [1024, 32], P('fsdp')
- gate_gradient: float32 [32, 1024, 512], P('expert', 'fsdp')
- up_gradient: float32 [32, 1024, 512], P('expert', 'fsdp')
- down_gradient: float32 [32, 512, 1024], P('expert', 'fsdp')
The draws below stay inside these ranges and needn't reach their ends.
Inputs may be any that keep to these rules, and one draw needn't show every extreme that they name: `segments`: within each sequence of 768 tokens the numbers never fall; number 1 begins within the sequence's first 192 tokens and number 2 within its last 192, so numbers 0 and 2 are never empty. `routes`: each row names 8 different experts; in the rows of one device (aligned blocks of 192 rows) no expert is named more than 72 times, a bound that some block reaches.
All inputs are finite; a program needn't handle non-finite values.
Results may differ from the reference program's by a relative error of at most 0.025.
Values may be sent and summed in bfloat16 or wider, within the bound.
No kernel may reach another device: no remote copies, remote signals or barrier semaphores. Data moves between devices by JAX's collectives and lax.ppermute only.
A program may use at most 192 MiB of HBM per device.

```python
import math
import jax
import jax.numpy as jnp
import numpy as np
from jax import lax

D = 1024
HEADS = 16
KV_HEADS = 8
HEAD = 64
FF = 512
TOP = 8
TOK_DEV = 192
EXPERTS = 32
SEQ = 768
TOKENS = 24576
CAP = 72
KV_WIDTH = 512


def draw_segments(key, part):
    key = jax.random.fold_in(key, 7)
    first_key, second_key = jax.random.split(key)
    sequences = TOKENS // SEQ
    starts = jax.random.randint(first_key, (sequences, 1), 1, TOK_DEV)
    finish = jax.random.randint(second_key, (sequences, 1), SEQ - TOK_DEV + 1, SEQ)
    places = jnp.arange(SEQ, dtype=jnp.int32)[None, :]
    numbers = (places >= starts).astype(jnp.int32) + (places >= finish).astype(jnp.int32)
    return numbers.reshape(TOKENS)


def block_scale(key, extent, cuts, low, top_value):
    level = 1.0
    for axis_at, shards_of in cuts:
        draws = jax.random.uniform(jax.random.fold_in(jax.random.fold_in(key, 6), axis_at), (shards_of,), jnp.float32, low / len(cuts), top_value / len(cuts))
        level = level * jnp.repeat(jnp.exp(draws), extent[axis_at] // shards_of).reshape((-1,) + (1,) * (len(extent) - 1 - axis_at))
    return level


def shared_out(key, own, number, rows, amount, top, bound, skew):
    sequence = jax.random.permutation(key, amount)
    heavy_load, usual = shares(amount, rows * top, bound, skew, True), shares(amount, rows * top, bound, skew, False)
    places = jnp.arange(amount)

    def named(lengths, rotation):
        used = int((lengths > 0).sum())
        fixed = max(1, used // 4)
        moved = fixed + (places - fixed + rotation * (used - fixed)) % max(1, amount - fixed)
        return jnp.zeros((amount,), jnp.int32).at[sequence[jnp.where(places < fixed, places, moved)]].set(jnp.asarray(lengths, jnp.int32))

    lengths = jnp.where(number % 4 == 0, named(heavy_load, number // 4), named(usual, number - number // 4 - 1))
    mixed = jax.random.permutation(jax.random.fold_in(own, 3), amount)
    giver, receiver = mixed[0:amount // 2 * 2:2], mixed[1:amount // 2 * 2:2]
    margin = jnp.minimum(lengths[giver] - 1, bound - lengths[receiver]) // 2
    margin = jnp.where((giver == sequence[0]) | (receiver == sequence[0]) | (lengths[receiver] == 0), 0, jnp.maximum(margin, 0))
    moved = jax.random.randint(jax.random.fold_in(own, 4), (amount // 2,), 0, 1 << 20) % (margin + 1)
    lengths = lengths.at[giver].add(-moved).at[receiver].add(moved)
    members = jnp.searchsorted(jnp.cumsum(lengths), jnp.arange(rows * top), side="right").astype(jnp.int32)
    grid = members.reshape(top, rows).T
    grid = grid[jax.random.permutation(jax.random.fold_in(own, 1), rows)]
    rotation = jax.random.randint(jax.random.fold_in(own, 2), (rows, 1), 0, top)
    return jnp.take_along_axis(grid, (jnp.arange(top)[None, :] + rotation) % top, axis=1)


def shares(count, total, bound, skew, full):
    loads = [(1 << 20) // math.isqrt(grade ** skew) + 1 for grade in range(1, count + 1)]
    largest = bound if full else min(bound, max(-(-total // count), total * loads[0] // sum(loads)))
    least = 1 if total - largest >= count - 1 else 0
    given, surplus = [largest] + [least] * (count - 1), total - largest - least * (count - 1)
    while surplus > 0:
        movable = [i for i in range(1, count) if given[i] < largest] or [i for i in range(1, count) if given[i] < bound]
        mass, left = sum([loads[i] for i in movable]), surplus
        for i in movable:
            extra = min(bound - given[i], max(1, left * loads[i] // mass), surplus)
            given[i] = given[i] + extra
            surplus = surplus - extra
    return np.array(given)


def centred(own_key, extent, deviation, bound, cuts=(), held_as=jnp.bfloat16):
    values = deviation * jax.random.normal(own_key, extent, jnp.float32)
    if cuts:
        values = values * block_scale(own_key, extent, cuts, -0.22, 0.18)
    return jnp.clip(values, -bound, bound).astype(held_as)


def setup_inputs(seed: int = 0) -> dict:
    streams_of = jax.random.split(jax.random.key(seed), 15)
    hidden = centred(streams_of[0], (TOKENS, D), 1.0, 6.0, ((0, 128),))
    segments = draw_segments(jax.random.fold_in(streams_of[14], 71), 0)
    routes_keys = jax.random.split(jax.random.fold_in(streams_of[2], 1), TOKENS // TOK_DEV)
    routes_turns = jax.random.permutation(jax.random.fold_in(streams_of[2], 3), TOKENS // TOK_DEV)
    routes = jax.vmap(lambda own, number: shared_out(jax.random.fold_in(streams_of[2], 2), own, number, TOK_DEV, EXPERTS, TOP, CAP, 2))(routes_keys, routes_turns).reshape((TOKENS, TOP))
    attention_gain = jnp.clip(1.0 + 0.15 * jax.random.normal(streams_of[3], (D,), jnp.float32), 0.25, 1.75).astype(jnp.bfloat16)
    query_weight = centred(streams_of[4], (D, D), D ** -0.5, 0.1875, ((0, 4),))
    key_weight = centred(streams_of[5], (D, KV_WIDTH), D ** -0.5, 0.1875, ((0, 4),))
    value_weight = centred(streams_of[6], (D, KV_WIDTH), D ** -0.5, 0.1875, ((0, 4),))
    projection_weight = centred(streams_of[7], (D, D), (D // 32) ** -0.5, 1.0, ((0, 4),))
    mixture_gain = jnp.clip(1.0 + 0.15 * jax.random.normal(streams_of[8], (D,), jnp.float32), 0.25, 1.75).astype(jnp.bfloat16)
    router_weight = centred(streams_of[9], (D, EXPERTS), (4 * D) ** -0.5, 0.09375, ((0, 4),))
    gate_weight = centred(streams_of[10], (EXPERTS, D, FF), D ** -0.5, 0.1875, ((0, 32), (1, 4)))
    up_weight = centred(streams_of[11], (EXPERTS, D, FF), D ** -0.5, 0.1875, ((0, 32), (1, 4)))
    down_weight = centred(streams_of[12], (EXPERTS, FF, D), (FF // 16) ** -0.5, 1.0, ((0, 32), (1, 4)))
    cotangent = centred(streams_of[13], (TOKENS, D), 1.0, 6.0, ((0, 128),))
    return {"hidden": hidden, "segments": segments, "routes": routes, "attention_gain": attention_gain, "query_weight": query_weight, "key_weight": key_weight, "value_weight": value_weight, "projection_weight": projection_weight, "mixture_gain": mixture_gain, "router_weight": router_weight, "gate_weight": gate_weight, "up_weight": up_weight, "down_weight": down_weight, "cotangent": cotangent}


@jax.custom_vjp
def low(v):
    return lax.optimization_barrier(v.astype(jnp.bfloat16)).astype(jnp.float32)

@jax.custom_vjp
def low_back(v):
    return v

def low_keep(v):
    return (low(v), None)

def low_pass(kept, grad):
    return (grad,)

def back_keep(v):
    return (v, None)

def back_low(kept, grad):
    return (low(grad),)
low.defvjp(low_keep, low_pass)
low_back.defvjp(back_keep, back_low)
epsilon = 1e-06
base_theta = 10000.0
highest_precision = lax.Precision.HIGHEST

def rotary_tables(positions):
    halves = jnp.arange(HEAD // 2, dtype=jnp.int32).astype(jnp.float32)
    frequencies = base_theta ** (-2.0 * halves / HEAD)
    angles = positions.astype(jnp.float32)[:, None] * frequencies[None, :]
    angles = jnp.concatenate([angles, angles], axis=1)
    return (jnp.cos(angles)[:, None, :], jnp.sin(angles)[:, None, :])

def half_turn(values):
    first, second = jnp.split(values, 2, axis=-1)
    return jnp.concatenate([-second, first], axis=-1)

def rotate(values, cosines, sines):
    return values * cosines + half_turn(values) * sines

def normalize(values, gain):
    scaling = lax.rsqrt(lax.optimization_barrier(jnp.mean(values * values, axis=-1, keepdims=True)) + epsilon)
    return values * scaling * gain

def slot_tables(routes):
    blocks = routes.reshape(TOKENS // TOK_DEV, TOK_DEV * TOP)

    def single(flat_routes):
        onehot = (flat_routes[:, None] == jnp.arange(EXPERTS, dtype=jnp.int32)[None, :]).astype(jnp.int32)
        slot_rank = lax.optimization_barrier(jnp.sum((jnp.cumsum(onehot, axis=0) - 1) * onehot, axis=1)).astype(jnp.int32)
        target = flat_routes * CAP + slot_rank
        return jnp.full((EXPERTS * CAP,), TOK_DEV * TOP, jnp.int32).at[target].set(jnp.arange(TOK_DEV * TOP, dtype=jnp.int32))
    return jax.vmap(single)(blocks)

def attend(pieces):
    queries, key_row_block, value_row_block, marks = pieces
    grouped_queries = queries.reshape(SEQ, KV_HEADS, HEADS // KV_HEADS, HEAD)
    raw_scores = jnp.einsum('abyx,jbx->byaj', grouped_queries, key_row_block, precision=highest_precision)
    scores = low_back(raw_scores * HEAD ** (-0.5))
    places = jnp.arange(SEQ, dtype=jnp.int32)
    visible = (places[None, :] <= places[:, None]) & (marks[None, :] == marks[:, None])
    scores = jnp.where(visible[None, None], scores, -1e+30)
    row_max = lax.optimization_barrier(jnp.max(scores, axis=-1, keepdims=True))
    weights = jnp.exp(scores - row_max)
    attention_probabilities = low(weights / lax.optimization_barrier(jnp.sum(weights, axis=-1, keepdims=True)))
    attention_mixed = jnp.einsum('icav,vie->aice', attention_probabilities, value_row_block, precision=highest_precision)
    return attention_mixed.reshape(SEQ, HEADS * HEAD)

def experts_block(pieces, gate_full, up_full, down_full):
    block_input, block_gates, table = pieces
    padded = jnp.concatenate([block_input, jnp.zeros((1, D), block_input.dtype)], axis=0)
    token_slot = table // TOP
    rows = low_back(padded[token_slot].reshape(EXPERTS, CAP, D))
    gate_values = low_back(jnp.einsum('ecd,edf->ecf', rows, gate_full, precision=highest_precision))
    up_values = low_back(jnp.einsum('ecd,edf->ecf', rows, up_full, precision=highest_precision))
    inner = low(jax.nn.silu(gate_values) * up_values)
    produced = low(low_back(jnp.einsum('ecf,efd->ecd', inner, down_full, precision=highest_precision)))
    gate_pad = jnp.concatenate([block_gates.reshape(-1), jnp.zeros((1,), block_gates.dtype)])
    weighted = gate_pad[table][:, None] * produced.reshape(EXPERTS * CAP, D)
    summed = jnp.zeros((TOK_DEV + 1, D), weighted.dtype).at[token_slot].add(weighted)
    return summed[:TOK_DEV]

def reference(hidden, segments, routes, attention_gain, query_weight, key_weight, value_weight, projection_weight, mixture_gain, router_weight, gate_weight, up_weight, down_weight, cotangent):
    tables = slot_tables(routes)
    selectors = (routes[:, :, None] == jnp.arange(EXPERTS, dtype=jnp.int32)[None, None, :]).astype(jnp.float32)
    cosines, sines = rotary_tables(jnp.arange(TOKENS, dtype=jnp.int32) % SEQ)
    sequences = TOKENS // SEQ
    blocks = TOKENS // TOK_DEV

    def layer(residual, gain_one, query_full, key_full, value_full, projection_full, gain_two, router_full, gate_full, up_full, down_full):
        activations = low(normalize(residual, gain_one))
        query_linear = low_back(jnp.dot(activations, query_full, precision=highest_precision)).reshape(TOKENS, HEADS, HEAD)
        key_linear = low_back(jnp.dot(activations, key_full, precision=highest_precision)).reshape(TOKENS, KV_HEADS, HEAD)
        value_row_block = low(low_back(jnp.dot(activations, value_full, precision=highest_precision))).reshape(TOKENS, KV_HEADS, HEAD)
        queries = low(rotate(query_linear, cosines, sines))
        key_row_block = low(rotate(key_linear, cosines, sines))
        mixed_rows = lax.map(jax.checkpoint(attend), (queries.reshape(sequences, SEQ, HEADS, HEAD), key_row_block.reshape(sequences, SEQ, KV_HEADS, HEAD), value_row_block.reshape(sequences, SEQ, KV_HEADS, HEAD), segments.reshape(sequences, SEQ)))
        mixed_rows = low(low_back(mixed_rows.reshape(TOKENS, HEADS * HEAD)))
        residual_two = residual + low_back(jnp.dot(mixed_rows, projection_full, precision=highest_precision))
        expert_input = low(normalize(residual_two, gain_two))
        logits = low_back(jnp.dot(expert_input, router_full, precision=highest_precision))
        chosen = lax.optimization_barrier(jnp.sum(selectors * logits[:, None, :], axis=2))
        chosen_max = lax.optimization_barrier(jnp.max(chosen, axis=1, keepdims=True))
        exponents = jnp.exp(chosen - chosen_max)
        gate_weights = exponents / lax.optimization_barrier(jnp.sum(exponents, axis=1, keepdims=True))

        def block_mix(pieces):
            return experts_block(pieces, gate_full, up_full, down_full)
        expert_mix = lax.map(jax.checkpoint(block_mix), (expert_input.reshape(blocks, TOK_DEV, D), gate_weights.reshape(blocks, TOK_DEV, TOP), tables))
        return residual_two + expert_mix.reshape(TOKENS, D)
    result, pullback = jax.vjp(layer, hidden.astype(jnp.float32), attention_gain.astype(jnp.float32), query_weight.astype(jnp.float32), key_weight.astype(jnp.float32), value_weight.astype(jnp.float32), projection_weight.astype(jnp.float32), mixture_gain.astype(jnp.float32), router_weight.astype(jnp.float32), gate_weight.astype(jnp.float32), up_weight.astype(jnp.float32), down_weight.astype(jnp.float32))
    gradients = pullback(cotangent.astype(jnp.float32))
    return (result.astype(jnp.bfloat16), gradients[0], gradients[1], gradients[2], gradients[3], gradients[4], gradients[5], gradients[6], gradients[7], gradients[8], gradients[9], gradients[10])
```

```python
import jax
import jax.numpy as jnp
from jax import lax
from jax.experimental import pallas as pl
from jax.experimental.pallas import tpu as pltpu
from jax.sharding import PartitionSpec as P

D = 1024
HEADS = 16
KV_HEADS = 8
HEAD = 64
FF = 512
TOP = 8
EXPERTS = 32
TOK = 192
CAP = 72
RING = 4

epsilon = 1e-06
base_theta = 10000.0
bf16 = jnp.bfloat16
f32 = jnp.float32


def place(z, x, core):
    return (z * RING + x) * 2 + core


def plane_perm(line, shift):
    pairs = []
    for z in range(RING):
        for x in range(RING):
            for core in range(2):
                if (core == 0) == (line == 0):
                    to = place(z, (x + shift) % RING, core)
                else:
                    to = place((z + shift) % RING, x, core)
                pairs.append((place(z, x, core), to))
    return pairs


def send_plane(value, line, shift):
    return lax.ppermute(value, "expert", plane_perm(line, shift % RING))


def send_core(value):
    return lax.ppermute(value, "expert", [(i, i ^ 1) for i in range(EXPERTS)])


def send_y(value, shift):
    return lax.ppermute(value, "fsdp", [(i, (i + shift) % RING) for i in range(RING)])


def dot(left, right):
    return jnp.dot(left, right, preferred_element_type=f32)


def contract_rows(left, right):
    return lax.dot_general(left, right, (((0,), (0,)), ((), ())), preferred_element_type=f32)


def contract_last(left, right):
    return lax.dot_general(left, right, (((1,), (1,)), ((), ())), preferred_element_type=f32)


def half_turn(values):
    first, second = jnp.split(values, 2, axis=-1)
    return jnp.concatenate([-second, first], axis=-1)


def rotate(values, cosines, sines):
    return values * cosines + half_turn(values) * sines


def rotate_back(deltas, cosines, sines):
    return deltas * cosines - half_turn(deltas * sines)


def scale_of(values):
    return lax.rsqrt(jnp.mean(values * values, axis=-1, keepdims=True) + epsilon)


def pick(blocks, index):
    return lax.dynamic_index_in_dim(blocks, index, 0, keepdims=False)


def in_order(received, position):
    own, one, two, three = received
    line = jnp.stack([three, two, one, own, three, two, one])
    return lax.dynamic_slice_in_dim(line, (3 - position) % RING, RING, 0)


def expert_kernel(groups, *refs):
    count = len(groups)
    x_refs, c_refs = refs[:count], refs[count : 2 * count]
    (slot_lane, slot_col, gate_lane, gate_w, up_w, down_w) = refs[2 * count : 2 * count + 6]
    outs = refs[2 * count + 6 :]
    delta_refs = outs[:count]
    gd_ref, xs_ref, cs_ref, inner_ref, dg_ref, du_ref = outs[count:]
    sources = [(g, k) for g in range(count) for k in range(groups[g])]
    rows = 2 * CAP
    slot_at = lax.broadcasted_iota(jnp.int32, (rows, TOK), 0)
    lane_at = lax.broadcasted_iota(jnp.int32, (TOK, rows), 1)
    picks, x_parts, c_parts, weights = [], [], [], []
    for s, (g, k) in enumerate(sources):
        first, second = slot_lane[s, 0:1, :], slot_lane[s, 1:2, :] + CAP
        upper = slot_at < CAP
        chosen_f = (slot_at == jnp.where(upper, first, second)).astype(f32)
        weight = jnp.where(upper, gate_lane[s, 0:1, :], gate_lane[s, 1:2, :])
        weights.append(jnp.sum(chosen_f * weight, axis=1, keepdims=True))
        picks.append(chosen_f)
        chosen_b = chosen_f.astype(bf16)
        x_parts.append(dot(chosen_b, x_refs[g][k * TOK : (k + 1) * TOK, :]))
        c_parts.append(dot(chosen_b, c_refs[g][k * TOK : (k + 1) * TOK, :]))
    back = []
    for e in range(2):
        span = slice(e * CAP, (e + 1) * CAP)
        xs = jnp.concatenate([part[span] for part in x_parts], axis=0).astype(bf16)
        cs = jnp.concatenate([part[span] for part in c_parts], axis=0).astype(bf16)
        weight = jnp.concatenate([part[span] for part in weights], axis=0)
        xs_ref[e] = xs
        cs_ref[e] = cs
        gate_values = dot(xs, gate_w[e])
        up_values = dot(xs, up_w[e])
        inner_delta = contract_last(cs, down_w[e])
        sigmoid = jax.nn.sigmoid(gate_values)
        silu = gate_values * sigmoid
        inner = silu * up_values
        gate_delta = jnp.sum(inner * inner_delta, axis=1, keepdims=True)
        inner_ref[e] = (inner * weight).astype(bf16)
        inner_delta = inner_delta * weight
        dg = (inner_delta * up_values * sigmoid * (1.0 + gate_values * (1.0 - sigmoid))).astype(bf16)
        du = (inner_delta * silu).astype(bf16)
        dg_ref[e] = dg
        du_ref[e] = du
        back.append(contract_last(dg, gate_w[e]) + contract_last(du, up_w[e]))
        for s in range(len(sources)):
            own = picks[s][span] * gate_delta[s * CAP : (s + 1) * CAP]
            gd_ref[s, e : e + 1, :] = jnp.sum(own, axis=0, keepdims=True)
    for s, (g, k) in enumerate(sources):
        first, second = slot_col[s, :, 0:1], slot_col[s, :, 1:2] + CAP
        scatter = (lane_at == jnp.where(lane_at < CAP, first, second)).astype(f32).astype(bf16)
        span = slice(s * CAP, (s + 1) * CAP)
        part = jnp.concatenate([back[0][span], back[1][span]], axis=0).astype(bf16)
        delta_refs[g][k * TOK : (k + 1) * TOK, :] = dot(scatter, part).astype(bf16)


def expert_call(xs, cs, slot_lane, slot_col, gate_lane, gate_w, up_w, down_w):
    groups = tuple(x.shape[0] // TOK for x in xs)
    sources = sum(groups)
    slots = sources * CAP
    shapes = [jax.ShapeDtypeStruct(x.shape, bf16) for x in xs]
    shapes += [
        jax.ShapeDtypeStruct((sources, 2, TOK), f32),
        jax.ShapeDtypeStruct((2, slots, D), bf16),
        jax.ShapeDtypeStruct((2, slots, D), bf16),
        jax.ShapeDtypeStruct((2, slots, FF), bf16),
        jax.ShapeDtypeStruct((2, slots, FF), bf16),
        jax.ShapeDtypeStruct((2, slots, FF), bf16),
    ]
    count = len(xs)
    out = pl.pallas_call(
        lambda *refs: expert_kernel(groups, *refs),
        out_shape=shapes,
        in_specs=[pl.BlockSpec(memory_space=pltpu.VMEM)] * (2 * count + 6),
        out_specs=[pl.BlockSpec(memory_space=pltpu.VMEM)] * len(shapes),
        compiler_params=pltpu.CompilerParams(vmem_limit_bytes=48 * 1024 * 1024),
        cost_estimate=pl.CostEstimate(
            flops=2 * 2 * slots * D * FF * 7, bytes_accessed=18_000_000, transcendentals=2 * slots * FF
        ),
    )(*xs, *cs, slot_lane, slot_col, gate_lane, gate_w, up_w, down_w)
    return out[:count], out[count:]


def output_kernel(groups, inner_ref, slot_col, down_w, *outs):
    rows = 2 * CAP
    lane_at = lax.broadcasted_iota(jnp.int32, (TOK, rows), 1)
    produced = [dot(inner_ref[e], down_w[e]) for e in range(2)]
    sources = [(g, k) for g in range(len(groups)) for k in range(groups[g])]
    for s, (g, k) in enumerate(sources):
        first, second = slot_col[s, :, 0:1], slot_col[s, :, 1:2] + CAP
        scatter = (lane_at == jnp.where(lane_at < CAP, first, second)).astype(f32).astype(bf16)
        span = slice(s * CAP, (s + 1) * CAP)
        part = jnp.concatenate([produced[0][span], produced[1][span]], axis=0).astype(bf16)
        outs[g][k * TOK : (k + 1) * TOK, :] = dot(scatter, part).astype(bf16)


def output_call(groups, inner, slot_col, down_w):
    shapes = [jax.ShapeDtypeStruct((g * TOK, D), bf16) for g in groups]
    return pl.pallas_call(
        lambda *refs: output_kernel(groups, *refs),
        out_shape=shapes,
        in_specs=[pl.BlockSpec(memory_space=pltpu.VMEM)] * 3,
        out_specs=[pl.BlockSpec(memory_space=pltpu.VMEM)] * len(shapes),
        compiler_params=pltpu.CompilerParams(vmem_limit_bytes=32 * 1024 * 1024),
        cost_estimate=pl.CostEstimate(
            flops=2 * 2 * inner.shape[1] * D * FF * 2, bytes_accessed=6_000_000, transcendentals=0
        ),
    )(inner, slot_col, down_w)


def gather_plane(block):
    line = jnp.concatenate([block] + [send_plane(block, 0, d) for d in (1, 2, 3)], axis=0)
    half = 2 * TOK
    one = send_plane(line, 1, 1)
    three = send_plane(line, 1, 3)
    two_low = send_plane(one[:half], 1, 1)
    two_high = send_plane(three[half:], 1, 3)
    return [line], [one], [two_low, two_high], [three]


def scatter_plane(own, one, two, three):
    half = 2 * TOK
    low = send_plane(two[0], 1, 3)
    high = send_plane(two[1], 1, 1)
    one = jnp.concatenate([(one[0][:half].astype(f32) + low.astype(f32)).astype(bf16), one[0][half:]], axis=0)
    three = jnp.concatenate([three[0][:half], (three[0][half:].astype(f32) + high.astype(f32)).astype(bf16)], axis=0)
    from_one = send_plane(one, 1, 3)
    from_three = send_plane(three, 1, 1)
    total = (own[0].astype(f32) + from_one.astype(f32) + from_three.astype(f32)).astype(bf16)
    parts = [total[d * TOK : (d + 1) * TOK] for d in range(RING)]
    parts = [parts[0]] + [send_plane(parts[d], 0, -d) for d in (1, 2, 3)]
    return sum(part.astype(f32) for part in parts)


def sum_plane(blocks, core, along, across):
    blocks = blocks.reshape((2, RING, RING) + blocks.shape[1:])
    other = send_core(pick(blocks, 1 - core))
    blocks = (pick(blocks, core).astype(f32) + other.astype(f32)).astype(bf16)
    for line, position in ((0, along), (1, across)):
        parts = [pick(blocks, position)]
        parts += [send_plane(pick(blocks, (position + d) % RING), line, d) for d in (1, 2, 3)]
        total = sum(part.astype(f32) for part in parts)
        blocks = total.astype(bf16)
    return total


def spread_plane(block, core, along, across):
    for line, position in ((1, across), (0, along)):
        block = in_order([block] + [send_plane(block, line, d) for d in (1, 2, 3)], position)
    other = send_core(block)
    low, high = jnp.where(core == 0, block, other), jnp.where(core == 0, other, block)
    both = jnp.stack([low, high])
    return both.reshape((EXPERTS,) + both.shape[3:])


def body(
    hidden,
    segments,
    routes,
    attention_gain,
    query_weight,
    key_weight,
    value_weight,
    projection_weight,
    mixture_gain,
    router_weight,
    gate_weight,
    up_weight,
    down_weight,
    cotangent,
):
    me = lax.axis_index("expert")
    mine = lax.axis_index("fsdp")
    core = me % 2
    chip = me // 2
    place_z, place_x = chip // RING, chip % RING
    along = jnp.where(core == 0, place_x, place_z)
    across = jnp.where(core == 0, place_z, place_x)
    groups = [[2 * i + c for i in range(EXPERTS // 2)] for c in range(2)]

    steps = jnp.arange(16, dtype=jnp.int32)
    from_across, from_along = (across - steps // RING) % RING, (along - steps % RING) % RING
    source_chip = jnp.where(core == 0, from_across * RING + from_along, from_along * RING + from_across)
    back_z, back_x = (place_z - steps // RING) % RING, (place_x - steps % RING) % RING
    source_step = jnp.where(core == 0, back_z * RING + back_x, back_x * RING + back_z)

    def trade(values):
        return lax.all_to_all(values, "expert", 0, 0, axis_index_groups=groups, tiled=True)

    hidden_blocks = [hidden] + [send_y(hidden, d) for d in (1, 2, 3)]
    segment_blocks = [segments] + [send_y(segments, d) for d in (1, 2, 3)]
    head_weights = jnp.concatenate(
        [w.reshape(256, RING, -1) for w in (query_weight, key_weight, value_weight)], axis=2
    ).transpose(1, 0, 2)
    own_heads = in_order(
        [pick(head_weights, mine)] + [send_y(pick(head_weights, (mine + d) % RING), d) for d in (1, 2, 3)], mine
    ).reshape(D, 512)
    gains = jnp.stack([attention_gain, mixture_gain])
    gains = in_order([gains] + [send_y(gains, d) for d in (1, 2, 3)], mine)
    gain_one = gains[:, 0].reshape(D).astype(f32)
    gain_two = gains[:, 1].reshape(D).astype(f32)

    named = (routes[:, :, None] == jnp.arange(EXPERTS, dtype=jnp.int32)[None, None, :]).astype(f32).sum(axis=1)
    lower = (jnp.arange(TOK)[:, None] > jnp.arange(TOK)[None, :]).astype(bf16)
    rank = dot(lower, named.astype(bf16)).astype(jnp.int32)
    slot = jnp.where(named > 0, rank, -1000)
    slot = trade(slot.T.reshape(16, 2, TOK))[source_chip]
    slot_lane = slot
    slot_col = slot.transpose(0, 2, 1)

    cot_blocks = gather_plane(cotangent)

    down_halves = down_weight[0].reshape(128, 2, 512).transpose(1, 0, 2).reshape(256, 512)
    pack = jnp.concatenate([gate_weight[0], up_weight[0], down_halves], axis=0)
    own_pack = in_order([pack] + [send_y(pack, d) for d in (1, 2, 3)], mine)
    other_pack = send_core(own_pack)
    packs = jnp.stack([jnp.where(core == 0, own_pack, other_pack), jnp.where(core == 0, other_pack, own_pack)])
    gate_full = packs[:, :, :256].reshape(2, D, FF)
    up_full = packs[:, :, 256:512].reshape(2, D, FF)
    down_full = packs[:, :, 512:].reshape(2, RING, 2, 128, 512).transpose(0, 1, 3, 2, 4).reshape(2, FF, D)

    projection = jnp.concatenate([projection_weight] + [send_y(projection_weight, -d) for d in (1, 2, 3)], axis=0)
    router = in_order([router_weight] + [send_y(router_weight, d) for d in (1, 2, 3)], mine).reshape(D, EXPERTS)

    x_all = jnp.concatenate(hidden_blocks, axis=0).astype(f32)
    segment_all = jnp.concatenate(segment_blocks, axis=0)
    order = (mine - jnp.arange(RING, dtype=jnp.int32)) % RING
    positions = (order[:, None] * TOK + jnp.arange(TOK, dtype=jnp.int32)[None, :]).reshape(-1)
    frequencies = base_theta ** (-2.0 * jnp.arange(HEAD // 2, dtype=jnp.int32).astype(f32) / HEAD)
    angles = positions.astype(f32)[:, None] * frequencies[None, :]
    angles = jnp.concatenate([angles, angles], axis=1)
    cosines, sines = jnp.cos(angles)[:, None, :], jnp.sin(angles)[:, None, :]
    scale_one = scale_of(x_all)
    activations = (x_all * scale_one * gain_one).astype(bf16)
    linear = dot(activations, own_heads)
    rows = RING * TOK
    queries = rotate(linear[:, :256].reshape(rows, 4, HEAD), cosines, sines).astype(bf16).reshape(rows, 2, 2, HEAD)
    keys = rotate(linear[:, 256:384].reshape(rows, 2, HEAD), cosines, sines).astype(bf16)
    values = linear[:, 384:].astype(bf16).reshape(rows, 2, HEAD)
    visible = (positions[None, :] <= positions[:, None]) & (segment_all[None, :] == segment_all[:, None])
    scaling = HEAD**-0.5
    scores = jnp.einsum("abyx,jbx->byaj", queries, keys, preferred_element_type=f32) * scaling
    scores = jnp.where(visible[None, None], scores, -1e30)
    exponents = jnp.exp(scores - jnp.max(scores, axis=-1, keepdims=True))
    unrounded = exponents / jnp.sum(exponents, axis=-1, keepdims=True)
    probabilities = unrounded.astype(bf16)
    mixed_heads = (
        jnp.einsum("icav,vie->aice", probabilities, values, preferred_element_type=f32)
        .reshape(rows, 256)
        .astype(bf16)
    )
    parts = [mixed_heads[r * TOK : (r + 1) * TOK] for r in range(RING)]
    mixed_rows = jnp.concatenate([parts[0]] + [send_y(parts[r], -r) for r in (1, 2, 3)], axis=1)
    residual = hidden.astype(f32)
    residual_two = residual + dot(mixed_rows, projection)
    scale_two = scale_of(residual_two)
    expert_input = (residual_two * scale_two * gain_two).astype(bf16)

    x_blocks = gather_plane(expert_input)
    logits = dot(expert_input, router)
    top_logit = jnp.max(jnp.where(named > 0, logits, -jnp.inf), axis=1, keepdims=True)
    gate_weights = jnp.where(named > 0, jnp.exp(jnp.where(named > 0, logits - top_logit, 0.0)), 0.0)
    gate_weights = gate_weights / jnp.sum(gate_weights, axis=1, keepdims=True)
    gate_lane = trade(gate_weights.T.reshape(16, 2, TOK))[source_chip]

    delta_parts, kept, out_parts = [], [], []
    for i in range(RING):
        span = slice(i * RING, (i + 1) * RING)
        delta_part, rest = expert_call(
            x_blocks[i], cot_blocks[i], slot_lane[span], slot_col[span], gate_lane[span], gate_full, up_full, down_full
        )
        delta_parts.append(delta_part)
        kept.append(rest)
    gate_delta = jnp.concatenate([rest[0] for rest in kept], axis=0)
    gate_delta = trade(gate_delta[source_step]).reshape(EXPERTS, TOK).T
    route_delta = scatter_plane(*delta_parts)
    for i in range(RING):
        span = slice(i * RING, (i + 1) * RING)
        sizes = tuple(x.shape[0] // TOK for x in x_blocks[i])
        out_parts.append(output_call(sizes, kept[i][3], slot_col[span], down_full))
    mixture = scatter_plane(*out_parts)
    output = (residual_two + mixture).astype(bf16)

    def expert_gradient(left, right):
        a = jnp.concatenate([rest[left] for rest in kept], axis=1)
        b = jnp.concatenate([rest[right] for rest in kept], axis=1)
        both = lax.dot_general(a, b, (((1,), (1,)), ((0,), (0,))), preferred_element_type=f32).astype(bf16)
        own = pick(both, core).astype(f32) + send_core(pick(both, 1 - core)).astype(f32)
        pieces = own.astype(bf16).reshape((RING, -1) + own.shape[1:])
        total = pick(pieces, mine).astype(f32)
        for d in (1, 2, 3):
            total = total + send_y(pick(pieces, (mine + d) % RING), d).astype(f32)
        return total[None]

    gate_gradient = expert_gradient(1, 4)
    up_gradient = expert_gradient(1, 5)
    down_gradient = expert_gradient(3, 2)

    mean_delta = jnp.sum(gate_weights * gate_delta, axis=1, keepdims=True)
    logit_delta = (gate_weights * (gate_delta - mean_delta)).astype(bf16)
    router_part = contract_rows(expert_input, logit_delta)
    input_delta = route_delta + contract_last(logit_delta, router)
    mixture_part = jnp.sum(input_delta * residual_two * scale_two, axis=0)
    inner = input_delta * gain_two
    upstream = cotangent.astype(f32)
    residual_delta = upstream + scale_two * (
        inner - residual_two * scale_two * scale_two * jnp.mean(inner * residual_two, axis=-1, keepdims=True)
    )
    attention_delta = residual_delta.astype(bf16)

    mixed_delta = contract_last(attention_delta, projection).astype(bf16)
    parts = [mixed_delta[:, r * 256 : (r + 1) * 256] for r in range(RING)]
    mixed_delta = jnp.concatenate([parts[0]] + [send_y(parts[r], r) for r in (1, 2, 3)], axis=0)
    mixed_delta = mixed_delta.reshape(rows, 2, 2, HEAD)
    probability_delta = jnp.einsum("abyx,jbx->byaj", mixed_delta, values, preferred_element_type=f32)
    row_delta = jnp.sum(probability_delta * unrounded, axis=-1, keepdims=True)
    score_delta = (unrounded * (probability_delta - row_delta)).astype(bf16)
    query_delta = jnp.einsum("icav,vie->aice", score_delta, keys, preferred_element_type=f32) * scaling
    key_delta = jnp.einsum("lapf,play->fly", score_delta, queries, preferred_element_type=f32) * scaling
    value_delta = jnp.einsum("lapf,play->fly", probabilities, mixed_delta, preferred_element_type=f32)
    query_delta = rotate_back(query_delta.reshape(rows, 4, HEAD), cosines, sines).reshape(rows, 256)
    key_delta = rotate_back(key_delta, cosines, sines).reshape(rows, 128)
    linear_delta = jnp.concatenate([query_delta, key_delta, value_delta.reshape(rows, 128)], axis=1).astype(bf16)

    attention_delta_all = jnp.concatenate(
        [attention_delta] + [send_y(attention_delta, d) for d in (1, 2, 3)], axis=0
    )
    projection_part = contract_rows(mixed_heads, attention_delta_all).astype(bf16)
    small = jnp.concatenate(
        [router_part, mixture_part[:, None], jnp.zeros((D, 128 - EXPERTS - 1), f32)], axis=1
    ).astype(bf16).reshape(RING, 256, 128)
    small = pick(small, mine).astype(f32) + sum(
        send_y(pick(small, (mine + d) % RING), d).astype(f32) for d in (1, 2, 3)
    )
    early = jnp.concatenate([projection_part, small.astype(bf16)], axis=1).reshape(EXPERTS, 8, D + 128)
    early = spread_plane(sum_plane(early, core, along, across).astype(bf16), core, along, across)
    early = early.reshape(256, D + 128).astype(f32)
    projection_gradient = early[:, :D]
    router_gradient = early[:, D : D + EXPERTS]
    mixture_gradient = early[:, D + EXPERTS]

    weight_part = contract_rows(activations, linear_delta)
    activation_part = contract_last(linear_delta, own_heads)
    gain_part = jnp.sum(activation_part * x_all * scale_one, axis=0)
    late = weight_part.reshape(RING, EXPERTS, 8, 512).transpose(1, 0, 2, 3).reshape(EXPERTS, 32, 512)
    gain_part = gain_part.reshape(RING, EXPERTS, 8).transpose(1, 0, 2)
    gain_rows = jnp.zeros((EXPERTS, 8, 512), f32).at[:, :RING, :8].set(gain_part)
    late = jnp.concatenate([late, gain_rows], axis=1).astype(bf16)
    late = sum_plane(late, core, along, across)
    pieces = jnp.concatenate(
        [late[:32].reshape(RING, 8, 512), jnp.broadcast_to(late[32:36, None], (RING, 8, 512))], axis=1
    ).astype(bf16)
    received = [pick(pieces, mine)] + [send_y(pick(pieces, (mine + d) % RING), d) for d in (1, 2, 3)]
    gain_sum = sum(part[8:].astype(f32) for part in received)
    pieces = in_order([part[:8] for part in received], mine).reshape(32, 512)
    late = spread_plane(jnp.concatenate([pieces, gain_sum.astype(bf16)], axis=0), core, along, across)
    attention_gradient = late[:, 32, :8].reshape(256).astype(f32)
    late = late[:, :32].reshape(EXPERTS, RING, 8, 512).transpose(0, 2, 1, 3).reshape(256, RING, 512).astype(f32)
    query_gradient = late[:, :, :256].reshape(256, D)
    key_gradient = late[:, :, 256:384].reshape(256, 512)
    value_gradient = late[:, :, 384:].reshape(256, 512)

    activation_part = activation_part.astype(bf16)
    parts = [activation_part[r * TOK : (r + 1) * TOK] for r in range(RING)]
    activation_delta = parts[0].astype(f32) + sum(send_y(parts[r], -r).astype(f32) for r in (1, 2, 3))
    own_scale = scale_one[:TOK]
    inner = activation_delta * gain_one
    input_gradient = residual_delta + own_scale * (
        inner - residual * own_scale * own_scale * jnp.mean(inner * residual, axis=-1, keepdims=True)
    )
    return (
        output,
        input_gradient,
        attention_gradient,
        query_gradient,
        key_gradient,
        value_gradient,
        projection_gradient,
        mixture_gradient,
        router_gradient,
        gate_gradient,
        up_gradient,
        down_gradient,
    )


def solution(mesh):
    rows = P(("expert", "fsdp"), None)
    weights = P("fsdp", None)
    experts = P("expert", "fsdp", None)
    return jax.shard_map(
        body,
        mesh=mesh,
        in_specs=(
            rows,
            P(("expert", "fsdp")),
            rows,
            P("fsdp"),
            weights,
            weights,
            weights,
            weights,
            P("fsdp"),
            weights,
            experts,
            experts,
            experts,
            rows,
        ),
        out_specs=(
            rows,
            rows,
            P("fsdp"),
            weights,
            weights,
            weights,
            weights,
            P("fsdp"),
            weights,
            experts,
            experts,
            experts,
        ),
        check_vma=False,
    )
```

```python
import jax
import jax.numpy as jnp
import numpy as np
from jax import lax
from jax.experimental import pallas as pl
from jax.experimental.pallas import tpu as pltpu
from jax.sharding import PartitionSpec as P

D = 1024
HEADS = 16
KV_HEADS = 8
HEAD = 64
FF = 512
TOP = 8
EXPERTS = 32
TOK = 192
CAP = 72
RING = 4
SEQ = RING * TOK
BLOCK = 256
SENT = TOK + 16
WIDE = D + 128
MIB = 1024 * 1024

epsilon = 1e-06
base_theta = 10000.0
bf16 = jnp.bfloat16
f32 = jnp.float32


def place(z, x, core):
    return (z * RING + x) * 2 + core


def plane_perm(line, shift):
    pairs = []
    for z in range(RING):
        for x in range(RING):
            for core in range(2):
                if (core == 0) == (line == 0):
                    to = place(z, (x + shift) % RING, core)
                else:
                    to = place((z + shift) % RING, x, core)
                pairs.append((place(z, x, core), to))
    return pairs


def send_plane(value, line, shift):
    return lax.ppermute(value, "expert", plane_perm(line, shift % RING))


def send_core(value):
    return lax.ppermute(value, "expert", [(i, i ^ 1) for i in range(EXPERTS)])


def send_y(value, shift):
    return lax.ppermute(value, "fsdp", [(i, (i + shift) % RING) for i in range(RING)])


def dot(left, right):
    return jnp.dot(left, right, preferred_element_type=f32)


def contract_rows(left, right):
    return lax.dot_general(left, right, (((0,), (0,)), ((), ())), preferred_element_type=f32)


def contract_last(left, right):
    return lax.dot_general(left, right, (((1,), (1,)), ((), ())), preferred_element_type=f32)


def scale_of(values):
    return lax.rsqrt(jnp.mean(values * values, axis=-1, keepdims=True) + epsilon)


def pick(blocks, index):
    return lax.dynamic_index_in_dim(blocks, index, 0, keepdims=False)


def in_order(received, position):
    own, one, two, three = received
    line = jnp.stack([three, two, one, own, three, two, one])
    return lax.dynamic_slice_in_dim(line, (3 - position) % RING, RING, 0)


def rotary_table():
    frequencies = base_theta ** (-2.0 * np.arange(HEAD // 2, dtype=np.float32) / np.float32(HEAD))
    angles = np.arange(SEQ, dtype=np.float32)[:, None] * frequencies.astype(np.float32)[None, :]
    angles = np.concatenate([angles] * 4, axis=1).astype(np.float32)
    return np.cos(angles).astype(np.float32), np.sin(angles).astype(np.float32)


def at_block(index, size):
    return pl.ds(pl.multiple_of(index * size, size), size)


VMEM = pl.BlockSpec(memory_space=pltpu.VMEM)
SMEM = pl.BlockSpec(memory_space=pltpu.SMEM)
HBM = pl.BlockSpec(memory_space=pltpu.HBM)


class Copies:
    def __init__(self, sems):
        self.sems, self.used = sems, 0

    def start(self, source, target):
        copy = pltpu.make_async_copy(source, target, self.sems.at[self.used])
        self.used += 1
        copy.start()
        return copy


def wait_all(copies):
    for copy in copies:
        copy.wait()


def turn(values, low_half):
    return jnp.where(low_half, -pltpu.roll(values, 96, 1), pltpu.roll(values, 32, 1))


def both_halves(pair):
    low = lax.broadcasted_iota(jnp.int32, pair.shape, 1) < HEAD
    swapped = pltpu.roll(pair, HEAD, 1)
    return jnp.where(low, pair, swapped).astype(bf16), jnp.where(low, swapped, pair).astype(bf16)


def one_half(pair, half):
    low = lax.broadcasted_iota(jnp.int32, pair.shape, 1) < HEAD
    return jnp.where(low == (half == 0), pair, jnp.zeros_like(pair))


def first_visible(place_at, starts):
    return jnp.where(place_at >= starts[1], starts[1], jnp.where(place_at >= starts[0], starts[0], 0))


def attention_kernel(mine, *refs):
    x_refs = refs[:4]
    cos_ref, sin_ref, proj_ref = refs[4:7]
    act_ref, qkv_ref, mixed_ref, part_ref, w_ref, start_ref, router_ref, gain_scr = refs[7:]
    router_ref[...] = jnp.zeros_like(router_ref)
    blocks = [jnp.bitwise_and(mine[0] - r, 3) for r in range(RING)]
    counts = jnp.zeros((1, 128), f32)
    for r in range(RING):
        notes = x_refs[r][TOK + 128 :, :].astype(f32)
        gain_scr[0:1, at_block(blocks[r], 256)] = notes[0:1, :256]
        counts = counts + notes[1:2, :128]
        router = [notes[8:16, 256 * q : 256 * (q + 1)] for q in range(4)]
        router_ref[:EXPERTS, at_block(blocks[r], 256)] = jnp.concatenate(router, axis=0).astype(bf16)
        w_ref[at_block(2 * blocks[r], 128), :] = x_refs[r][TOK : TOK + 128, :512]
        w_ref[at_block(2 * blocks[r] + 1, 128), :] = x_refs[r][TOK : TOK + 128, 512:]
    lanes = lax.broadcasted_iota(jnp.int32, (1, 128), 1)
    starts = [jnp.sum(jnp.where(lanes == i, counts, 0.0), axis=1, keepdims=True).astype(jnp.int32) for i in (0, 1)]
    start_ref[...] = jnp.broadcast_to(jnp.where(lanes == 0, starts[0], starts[1]), (8, 128))
    gain = gain_scr[0:1, :]
    for r in range(RING):
        x = x_refs[r][:TOK, :].astype(f32)
        act_ref[at_block(blocks[r], TOK), :] = (x * scale_of(x) * gain).astype(bf16)
    low = lax.broadcasted_iota(jnp.int32, (BLOCK, 128), 1) % HEAD < HEAD // 2
    for i in range(SEQ // BLOCK):
        span = slice(i * BLOCK, (i + 1) * BLOCK)
        linear = dot(act_ref[span, :], w_ref[...])
        for g in range(3):
            part = linear[:, g * 128 : (g + 1) * 128]
            part = part * cos_ref[span, :] + turn(part, low) * sin_ref[span, :]
            qkv_ref[span, g * 128 : (g + 1) * 128] = part.astype(bf16)
        qkv_ref[span, 384:] = linear[:, 384:].astype(bf16)
    keys = both_halves(qkv_ref[:, 256:384].astype(f32))
    values = both_halves(qkv_ref[:, 384:].astype(f32))
    values = [[one_half(v, h) for h in range(2)] for v in values]
    for i in range(SEQ // BLOCK):
        span, reach = slice(i * BLOCK, (i + 1) * BLOCK), (i + 1) * BLOCK
        query_at = lax.broadcasted_iota(jnp.int32, (BLOCK, 1), 0) + i * BLOCK
        key_at = lax.broadcasted_iota(jnp.int32, (BLOCK, reach), 1)
        visible = jnp.logical_and(key_at <= query_at, key_at >= first_visible(query_at, starts))
        bias = jnp.where(visible, 0.0, -1e30)
        for g in range(2):
            query = qkv_ref[span, g * 128 : (g + 1) * 128]
            total = jnp.zeros((BLOCK, 128), f32)
            for h in range(2):
                scores = contract_last(one_half(query, h), keys[g][:reach]) * HEAD**-0.5 + bias
                exponents = jnp.exp(scores - jnp.max(scores, axis=1, keepdims=True))
                scores = exponents * (1.0 / jnp.sum(exponents, axis=1, keepdims=True))
                total = total + dot(scores.astype(bf16), values[g][h][:reach])
            mixed_ref[span, g * 128 : (g + 1) * 128] = total.astype(bf16)
    for r in range(RING):
        part_ref[r] = dot(mixed_ref[at_block(blocks[r], TOK), :], proj_ref[...]).astype(bf16)


def attention_call(mine, xs, cosines, sines, projection):
    return pl.pallas_call(
        attention_kernel,
        out_shape=[
            jax.ShapeDtypeStruct((SEQ, D), bf16),
            jax.ShapeDtypeStruct((SEQ, 512), bf16),
            jax.ShapeDtypeStruct((SEQ, 256), bf16),
            jax.ShapeDtypeStruct((RING, TOK, D), bf16),
            jax.ShapeDtypeStruct((D, 512), bf16),
            jax.ShapeDtypeStruct((8, 128), jnp.int32),
            jax.ShapeDtypeStruct((128, D), bf16),
        ],
        in_specs=[SMEM] + [VMEM] * 7,
        out_specs=[VMEM] * 7,
        scratch_shapes=[pltpu.VMEM((8, D), f32)],
        compiler_params=pltpu.CompilerParams(vmem_limit_bytes=32 * MIB),
        cost_estimate=pl.CostEstimate(flops=8_000_000_000, bytes_accessed=8_000_000, transcendentals=2_000_000),
    )(mine, *xs, cosines, sines, projection)


def attention_back_kernel(mine, *refs):
    delta_hbm, x_hbm, held_hbm, (start_ref, mixture_ref) = refs[:4], refs[4:8], refs[8:16], refs[16:18]
    (own_hbm, other_hbm, weight_ref, part_ref, grad_ref, delta_scr, x_ref), held = refs[18:25], refs[25:33]
    (md_scr, dq_scr, dk_scr, dv_scr, ld_scr, grad_v, sems) = refs[33:]
    (proj_ref, qkv_ref, cos_ref, sin_ref, mixed_ref, small_ref, act_ref, w_ref) = held
    copies = Copies(sems)
    blocks = [jnp.bitwise_and(mine[0] - r, 3) for r in range(RING)]
    first = [copies.start(delta_hbm[r], delta_scr.at[at_block(blocks[r], TOK)]) for r in range(RING)]
    first += [copies.start(held_hbm[i], held[i]) for i in range(2)]
    later = [copies.start(held_hbm[i], held[i]) for i in range(2, 8)]
    later += [copies.start(x_hbm[r].at[pl.ds(0, TOK)], x_ref.at[r]) for r in range(RING)]
    grads = [copies.start(value, grad_v.at[i]) for i, value in enumerate((own_hbm, other_hbm))]
    wait_all(first)
    md_scr[...] = contract_last(delta_scr[...], proj_ref[...]).astype(bf16)
    starts = [start_ref[0:1, 0:1], start_ref[0:1, 1:2]]
    keys = both_halves(qkv_ref[:, 256:384].astype(f32))
    values = both_halves(qkv_ref[:, 384:].astype(f32))
    scaling = HEAD**-0.5
    dk_scr[...] = jnp.zeros_like(dk_scr)
    dv_scr[...] = jnp.zeros_like(dv_scr)
    for i in range(SEQ // BLOCK):
        span, reach = slice(i * BLOCK, (i + 1) * BLOCK), (i + 1) * BLOCK
        query_at = lax.broadcasted_iota(jnp.int32, (1, BLOCK), 1) + i * BLOCK
        key_at = lax.broadcasted_iota(jnp.int32, (reach, BLOCK), 0)
        visible = jnp.logical_and(key_at <= query_at, key_at >= first_visible(query_at, starts))
        bias = jnp.where(visible, 0.0, -1e30)
        for g in range(2):
            query = qkv_ref[span, g * 128 : (g + 1) * 128]
            delta = md_scr[span, g * 128 : (g + 1) * 128]
            dq = jnp.zeros((BLOCK, 128), f32)
            for h in range(2):
                own_query, own_delta = one_half(query, h), one_half(delta, h)
                scores = contract_last(keys[g][:reach], own_query) * scaling + bias
                exponents = jnp.exp(scores - jnp.max(scores, axis=0, keepdims=True))
                probability = exponents * (1.0 / jnp.sum(exponents, axis=0, keepdims=True))
                probability_delta = contract_last(values[g][:reach], own_delta)
                row_delta = jnp.sum(probability * probability_delta, axis=0, keepdims=True)
                score_delta = (probability * (probability_delta - row_delta)).astype(bf16)
                dk_scr[g, :reach, :] += dot(score_delta, own_query)
                dv_scr[g, :reach, :] += dot(probability.astype(bf16), own_delta)
                dq = dq + contract_rows(score_delta, one_half(keys[g][:reach], h))
            dq_scr[span, g * 128 : (g + 1) * 128] = dq * scaling
    low = lax.broadcasted_iota(jnp.int32, (SEQ, 128), 1) < HEAD
    turned = lax.broadcasted_iota(jnp.int32, (SEQ, 128), 1) % HEAD < HEAD // 2

    def folded(scr):
        first, second = scr[0], scr[1]
        first = first + pltpu.roll(first, HEAD, 1)
        second = second + pltpu.roll(second, HEAD, 1)
        return jnp.where(low, first, second)

    def back(values):
        return values * cos_ref[...] - turn(values * sin_ref[...], turned)

    wait_all(grads)
    for j in range(RING):
        grad_v[0, j] = (grad_v[0, j].astype(f32) + grad_v[1, j].astype(f32)).astype(bf16)
    sent = copies.start(grad_v.at[0], grad_ref)
    wait_all(later)
    for g in range(2):
        ld_scr[:, g * 128 : (g + 1) * 128] = back(dq_scr[:, g * 128 : (g + 1) * 128]).astype(bf16)
    ld_scr[:, 256:384] = back(folded(dk_scr) * scaling).astype(bf16)
    ld_scr[:, 384:] = folded(dv_scr).astype(bf16)
    gain = jnp.zeros((1, D), f32)
    for r in range(RING):
        part = contract_last(ld_scr[at_block(blocks[r], TOK), :], w_ref[...])
        part_ref[r] = part.astype(bf16)
        x = x_ref[r].astype(f32)
        gain = gain + jnp.sum(part * x * scale_of(x), axis=0, keepdims=True)
    lanes = lax.broadcasted_iota(jnp.int32, (256, 128), 1)
    for pair in range(2):
        rows = []
        for j in (2 * pair, 2 * pair + 1):
            span = slice(j * 256, (j + 1) * 256)
            first = jnp.broadcast_to(gain[:, span], (128, 256)).T
            second = jnp.broadcast_to(mixture_ref[:, span], (128, 256)).T
            side = jnp.where(lanes == 33, first, jnp.where(lanes == 32, second, small_ref[span, :]))
            both = jnp.concatenate([contract_rows(act_ref[:, span], ld_scr[...]), side], axis=1)
            rows.append(both.reshape(EXPERTS, 8, 640))
        weight_ref[:, 16 * pair : 16 * pair + 16, :] = jnp.concatenate(rows, axis=1).astype(bf16)
    part = contract_rows(mixed_ref[...], delta_scr[...]).reshape(EXPERTS, 8, D)
    part = jnp.concatenate([part[:, :, :512], part[:, :, 512:]], axis=1).astype(bf16)
    weight_ref[:, 32:, :512] = part
    weight_ref[:, 32:, 512:] = jnp.zeros((EXPERTS, 16, 128), bf16)
    sent.wait()


def attention_back_call(mine, deltas, xs, held, starts, mixture, grads):
    return pl.pallas_call(
        attention_back_kernel,
        out_shape=[
            jax.ShapeDtypeStruct((EXPERTS, 48, 640), bf16),
            jax.ShapeDtypeStruct((RING, TOK, D), bf16),
            jax.ShapeDtypeStruct(grads[0].shape, bf16),
        ],
        in_specs=[SMEM] + [HBM] * 16 + [VMEM] * 2 + [HBM] * 2,
        out_specs=[VMEM] * 2 + [HBM],
        scratch_shapes=[pltpu.VMEM((SEQ, D), bf16), pltpu.VMEM((RING, TOK, D), bf16)]
        + [pltpu.VMEM(value.shape, value.dtype) for value in held]
        + [
            pltpu.VMEM((SEQ, 256), bf16),
            pltpu.VMEM((SEQ, 256), f32),
            pltpu.VMEM((2, SEQ, 128), f32),
            pltpu.VMEM((2, SEQ, 128), f32),
            pltpu.VMEM((SEQ, 512), bf16),
            pltpu.VMEM((2,) + grads[0].shape, bf16),
            pltpu.SemaphoreType.DMA((32,)),
        ],
        compiler_params=pltpu.CompilerParams(vmem_limit_bytes=48 * MIB),
        cost_estimate=pl.CostEstimate(flops=100_000_000, bytes_accessed=100_000, transcendentals=0),
    )(mine, *deltas, *xs, *held, starts, mixture, *grads)


def load_weights(copies, packs, gate_w, up_w, down_w):
    gates, downs = [], []
    if gate_w is not None:
        for e in range(2):
            for r in range(RING):
                gates.append(copies.start(packs.at[e, r, 0:256], gate_w.at[e, r * 256 : (r + 1) * 256, :]))
                gates.append(copies.start(packs.at[e, r, 256:512], up_w.at[e, r * 256 : (r + 1) * 256, :]))
    for e in range(2):
        for r in range(RING):
            for half in range(2):
                target = down_w.at[e, r * 128 : (r + 1) * 128, half * 512 : (half + 1) * 512]
                downs.append(copies.start(packs.at[e, r, 512 + half * 128 : 640 + half * 128], target))
    return gates, downs


def expert_kernel(groups, out_groups, order, at, *refs):
    count, out_count = len(groups), len(out_groups)
    x_refs, refs = refs[:count], refs[count:]
    (cots, info_ref, packs), refs = refs[:3], refs[3:]
    sent_refs, refs = refs[:out_count], refs[out_count:]
    (xs_ref, dy_ref, inner_ref, dg_ref, du_ref), refs = refs[:5], refs[5:]
    (x_v, c_v, info_v, gate_w, up_w, down_w, sent_v, scatter_v), refs = refs[:8], refs[8:]
    (xs_v, dy_v, inner_v, dg_v, du_v, sems) = refs
    chip = at[18]
    copies = Copies(sems)
    sources = [(g, k) for g in range(count) for k in range(groups[g])]
    targets = [(g, k) for g in range(out_count) for k in range(out_groups[g])]
    ins = []
    for s, (g, k) in enumerate(sources):
        ins.append(
            [
                copies.start(info_ref.at[at[order[s]]], info_v.at[s]),
                copies.start(x_refs[g].at[pl.ds(k * TOK, TOK)], x_v.at[s]),
                copies.start(cots.at[at[order[s]]], c_v.at[s]),
            ]
        )
    gates_in, downs_in = load_weights(copies, packs, gate_w, up_w, down_w)
    rows = 2 * CAP
    upper = lax.broadcasted_iota(jnp.int32, (rows, 256), 0) < CAP
    pick_at = lax.broadcasted_iota(jnp.int32, (rows, 256), 0)
    pick_at = jnp.where(upper, pick_at, pick_at - CAP).astype(f32)
    tall_at = lax.broadcasted_iota(jnp.int32, (TOK, rows), 1)
    scatter_at = jnp.where(tall_at < CAP, tall_at, tall_at - CAP).astype(f32)
    kind = lax.broadcasted_iota(jnp.int32, (8, rows), 0)
    expert = jnp.where(lax.broadcasted_iota(jnp.int32, (8, rows), 1) < CAP, 0, 1)
    slot_of = (kind == expert).astype(f32).astype(bf16)
    x_parts, dy_parts, picks = [], [], []
    for s in range(len(sources)):
        wait_all(ins[s])
        info = info_v[s]
        pick = jnp.where(upper, info[0:1], info[1:2]) == pick_at
        picks.append(pick.astype(f32))
        chosen = picks[s][:, :TOK].astype(bf16)
        weighted = jnp.where(pick, jnp.where(upper, info[2:3], info[3:4]), 0.0)[:, :TOK].astype(bf16)
        info_b = info[:, :TOK].astype(bf16)
        scatter = contract_rows(info_b, slot_of) == scatter_at
        scatter_v[s] = scatter.astype(f32).astype(bf16)
        x_parts.append(dot(chosen, x_v[s]))
        dy_parts.append(dot(weighted, c_v[s]))
    out = []
    back, back_gate = [], []
    for e in range(2):
        span = slice(e * CAP, (e + 1) * CAP)
        xs = jnp.concatenate([part[span] for part in x_parts], axis=0).astype(bf16)
        xs_v[e] = xs
        out.append(copies.start(xs_v.at[e], xs_ref.at[e]))
        if e == 0:
            wait_all(gates_in)
        gate_values = dot(xs, gate_w[e])
        up_values = dot(xs, up_w[e])
        dy = jnp.concatenate([part[span] for part in dy_parts], axis=0).astype(bf16)
        dy_v[e] = dy
        out.append(copies.start(dy_v.at[e], dy_ref.at[e]))
        if e == 0:
            wait_all(downs_in)
        inner_delta = contract_last(dy, down_w[e])
        sigmoid = jax.nn.sigmoid(gate_values)
        silu = gate_values * sigmoid
        inner = silu * up_values
        inner_v[e] = inner.astype(bf16)
        back_gate.append(jnp.sum(inner * inner_delta, axis=1, keepdims=True))
        dg = (inner_delta * up_values * sigmoid * (1.0 + gate_values * (1.0 - sigmoid))).astype(bf16)
        du = (inner_delta * silu).astype(bf16)
        dg_v[e] = dg
        du_v[e] = du
        for value, ref in ((inner_v, inner_ref), (dg_v, dg_ref), (du_v, du_ref)):
            out.append(copies.start(value.at[e], ref.at[e]))
        back.append(contract_last(dg, gate_w[e]) + contract_last(du, up_w[e]))
    row_at = lax.broadcasted_iota(jnp.int32, (16, D), 0)
    for s, (g, k) in enumerate(targets):
        span = slice(s * CAP, (s + 1) * CAP)
        part = jnp.concatenate([back[0][span], back[1][span]], axis=0).astype(bf16)
        sent_v[s, :TOK, :] = dot(scatter_v[s], part).astype(bf16)
        own = [
            jnp.sum(picks[s][e * CAP : (e + 1) * CAP] * back_gate[e][span], axis=0, keepdims=True)
            for e in range(2)
        ]
        high = [value.astype(bf16).astype(f32) for value in own]
        row = jnp.concatenate(high + [own[e] - high[e] for e in range(2)], axis=1)
        sent_v[s, TOK:, :] = jnp.where(row_at == chip, row, 0.0).astype(bf16)
        out.append(copies.start(sent_v.at[s], sent_refs[g].at[pl.ds(k * SENT, SENT)]))
    wait_all(out)


def expert_call(order, at, xs, out_groups, cots, info, packs):
    groups = tuple(x.shape[0] // TOK for x in xs)
    sources = len(order)
    slots = sources * CAP
    count = len(xs)
    kept = [
        ((2, slots, D), bf16),
        ((2, slots, D), bf16),
        ((2, slots, FF), bf16),
        ((2, slots, FF), bf16),
        ((2, slots, FF), bf16),
    ]
    shapes = [jax.ShapeDtypeStruct((g * SENT, D), bf16) for g in out_groups]
    shapes += [jax.ShapeDtypeStruct(*entry) for entry in kept]
    out = pl.pallas_call(
        lambda *refs: expert_kernel(groups, out_groups, order, *refs),
        out_shape=shapes,
        in_specs=[SMEM] + [HBM] * (count + 3),
        out_specs=[HBM] * len(shapes),
        scratch_shapes=[
            pltpu.VMEM((sources, TOK, D), bf16),
            pltpu.VMEM((sources, TOK, D), bf16),
            pltpu.VMEM((sources, 8, 256), f32),
            pltpu.VMEM((2, D, FF), bf16),
            pltpu.VMEM((2, D, FF), bf16),
            pltpu.VMEM((2, FF, D), bf16),
            pltpu.VMEM((sources, SENT, D), bf16),
            pltpu.VMEM((sources, TOK, 2 * CAP), bf16),
        ]
        + [pltpu.VMEM(*entry) for entry in kept]
        + [pltpu.SemaphoreType.DMA((128,))],
        compiler_params=pltpu.CompilerParams(vmem_limit_bytes=58 * MIB),
        cost_estimate=pl.CostEstimate(
            flops=2 * 2 * slots * D * FF * 16, bytes_accessed=26_000_000, transcendentals=2 * slots * FF
        ),
    )(at, *xs, cots, info, packs)
    return out[: len(out_groups)], out[len(out_groups) :]


def produce_kernel(orders, at, *refs):
    count = len(orders)
    inner_refs, (packs, _, out_ref, inner_v, down_w, out_v, sems) = refs[:count], refs[count:]
    copies = Copies(sems)
    _, downs_in = load_weights(copies, packs, None, None, down_w)
    ins = [copies.start(inner_refs[i], inner_v.at[:, pl.ds(8 * i * CAP, 8 * CAP)]) for i in range(count)]
    wait_all(downs_in)
    outs = []
    for i, order in enumerate(orders):
        ins[i].wait()
        rows = slice(8 * i * CAP, 8 * (i + 1) * CAP)
        produced = [dot(inner_v[e, rows, :], down_w[e]) for e in range(2)]
        for s, source in enumerate(order):
            span = slice(s * CAP, (s + 1) * CAP)
            out_v[source] = jnp.concatenate([produced[0][span], produced[1][span]], axis=0).astype(bf16)
            outs.append(copies.start(out_v.at[source], out_ref.at[at[source]]))
    wait_all(outs)


def produce_call(orders, at, kept, packs, done):
    inners = [chunk[2] for chunk in kept]
    return pl.pallas_call(
        lambda *refs: produce_kernel(orders, *refs),
        out_shape=jax.ShapeDtypeStruct((16, 2 * CAP, D), bf16),
        in_specs=[SMEM] + [HBM] * (len(orders) + 2),
        out_specs=HBM,
        scratch_shapes=[
            pltpu.VMEM((2, 16 * CAP, FF), bf16),
            pltpu.VMEM((2, FF, D), bf16),
            pltpu.VMEM((16, 2 * CAP, D), bf16),
            pltpu.SemaphoreType.DMA((64,)),
        ],
        compiler_params=pltpu.CompilerParams(vmem_limit_bytes=40 * MIB),
        cost_estimate=pl.CostEstimate(
            flops=2 * 2 * 1152 * D * FF * 3, bytes_accessed=14_000_000, transcendentals=0
        ),
    )(at, *inners, packs, done)


def combine_kernel(slot_ref, gate_ref, residual_ref, rows_ref, out_ref, rows_v, sems):
    copies = Copies(sems)
    ins = [copies.start(rows_ref.at[p], rows_v.at[p]) for p in range(16)]
    lane = lax.broadcasted_iota(jnp.int32, (TOK, 2 * CAP), 1)
    slot_at = jnp.where(lane < CAP, lane, lane - CAP).astype(f32)
    at_row = lax.broadcasted_iota(jnp.int32, (128, 2 * CAP), 0)
    at_half = jnp.where(lax.broadcasted_iota(jnp.int32, (128, 2 * CAP), 1) < CAP, 0, 1)
    total = residual_ref[...]
    for p in range(16):
        own = (at_row == 2 * p + at_half).astype(f32).astype(bf16)
        here = dot(slot_ref[...], own) == slot_at
        weight = jnp.where(here, dot(gate_ref[...], own), 0.0).astype(bf16)
        ins[p].wait()
        total = total + dot(weight, rows_v[p])
    out_ref[...] = total.astype(bf16)


def combine_call(slots, gates, residual, rows):
    return pl.pallas_call(
        combine_kernel,
        out_shape=jax.ShapeDtypeStruct((TOK, D), bf16),
        in_specs=[VMEM] * 3 + [HBM],
        out_specs=VMEM,
        scratch_shapes=[pltpu.VMEM((16, 2 * CAP, D), bf16), pltpu.SemaphoreType.DMA((16,))],
        compiler_params=pltpu.CompilerParams(vmem_limit_bytes=24 * MIB),
        cost_estimate=pl.CostEstimate(flops=2_000_000_000, bytes_accessed=6_000_000, transcendentals=0),
    )(slots, gates, residual, rows)


def gradient_kernel(at, *refs):
    chunks = [refs[5 * i : 5 * i + 5] for i in range((len(refs) - 8) // 5)]
    own_ref, other_ref, xs_v, dy_v, inner_v, both_v, out_v, sems = refs[-8:]
    core = at[16]
    copies = Copies(sems)
    ins = []
    for e in range(2):
        gate_in, down_in, start = [], [], 0
        for xs, dy, inner, dg, du in chunks:
            span = pl.ds(start, xs.shape[1])
            start += xs.shape[1]
            gate_in.append(copies.start(xs.at[e], xs_v.at[e, span]))
            gate_in.append(copies.start(dg.at[e], both_v.at[e, span, 0:FF]))
            gate_in.append(copies.start(du.at[e], both_v.at[e, span, FF : 2 * FF]))
            down_in.append(copies.start(inner.at[e], inner_v.at[e, span]))
            down_in.append(copies.start(dy.at[e], dy_v.at[e, span]))
        ins.append((gate_in, down_in))
    outs = []
    for e in range(2):
        wait_all(ins[e][0])
        for j in range(RING):
            part = contract_rows(xs_v[e, :, j * 256 : (j + 1) * 256], both_v[e]).astype(bf16)
            out_v[e, j, 0:256, :] = part[:, :FF]
            out_v[e, j, 256:512, :] = part[:, FF:]
        wait_all(ins[e][1])
        for j in range(RING):
            part = contract_rows(inner_v[e, :, j * 128 : (j + 1) * 128], dy_v[e]).astype(bf16)
            out_v[e, j, 512:640, :] = part[:, :512]
            out_v[e, j, 640:768, :] = part[:, 512:]
    outs.append(copies.start(out_v.at[1 - core], other_ref))
    outs.append(copies.start(out_v.at[core], own_ref))
    wait_all(outs)


def gradient_call(at, kept):
    size = sum(chunk[0].shape[1] for chunk in kept)
    operands = [entry for chunk in kept for entry in chunk]
    return pl.pallas_call(
        gradient_kernel,
        out_shape=[jax.ShapeDtypeStruct((RING, 768, 512), bf16)] * 2,
        in_specs=[SMEM] + [HBM] * len(operands),
        out_specs=[HBM] * 2,
        scratch_shapes=[
            pltpu.VMEM((2, size, D), bf16),
            pltpu.VMEM((2, size, D), bf16),
            pltpu.VMEM((2, size, FF), bf16),
            pltpu.VMEM((2, size, 2 * FF), bf16),
            pltpu.VMEM((2, RING, 768, 512), bf16),
            pltpu.SemaphoreType.DMA((64,)),
        ],
        compiler_params=pltpu.CompilerParams(vmem_limit_bytes=58 * MIB),
        cost_estimate=pl.CostEstimate(
            flops=2 * 2 * 1152 * D * FF * 6, bytes_accessed=24_000_000, transcendentals=0
        ),
    )(at, *operands)


def gather_plane(own, info):
    near = [send_plane(own, 0, d) for d in (1, 2, 3)]
    own_one, own_three = send_plane(own, 1, 1), send_plane(own, 1, 3)
    rest = jnp.concatenate(near, axis=0)
    rest_one, rest_three = send_plane(rest, 1, 1), send_plane(rest, 1, 3)
    own_two = send_plane(own_one, 1, 1)
    held = 0 * info[0, 0, 0].astype(bf16)
    low_two = send_plane(rest_one[:TOK] + held, 1, 1)
    high_two = send_plane(rest_three[TOK:] + held, 1, 3)
    return [own] + near, [own_one, rest_one], [own_two, low_two, high_two], [own_three, rest_three]


def add(left, right):
    return (left.astype(f32) + right.astype(f32)).astype(bf16)


def scatter_plane(own, one, two, three, before):
    before = 0 * before[0, 0, 0].astype(f32)
    low = send_plane(two[0], 1, 3)
    high = send_plane(two[1], 1, 1)
    own_three = send_plane(three[0], 1, 1)
    rest_three = jnp.concatenate([three[1][:SENT], add(three[1][SENT:], high)], axis=0)
    rest_three = send_plane(rest_three, 1, 1)
    rest_one = jnp.concatenate([add(one[1][:SENT], low[SENT:]), one[1][SENT:]], axis=0)
    rest_one = send_plane(rest_one, 1, 3)
    own_one = send_plane(add(one[0], low[:SENT]), 1, 3)
    total = own[0].astype(f32) + own_one.astype(f32) + own_three.astype(f32)
    for d in (1, 2, 3):
        span = slice((d - 1) * SENT, d * SENT)
        part = own[d].astype(f32) + before + rest_one[span].astype(f32) + rest_three[span].astype(f32)
        total = total + send_plane(part.astype(bf16), 0, -d).astype(f32)
    return total


def sum_plane(blocks, core, along, across):
    blocks = blocks.reshape((2, RING, RING) + blocks.shape[1:])
    blocks = add(pick(blocks, core), send_core(pick(blocks, 1 - core)))
    blocks = jnp.where(core == 0, jnp.swapaxes(blocks, 0, 1), blocks)
    for line, position in ((0, along), (1, across)):
        parts = [pick(blocks, position)]
        parts += [send_plane(pick(blocks, (position + d) % RING), line, d) for d in (1, 2, 3)]
        total = sum(part.astype(f32) for part in parts)
        blocks = total.astype(bf16)
    return total


def spread_plane(block, core, along, across, done):
    for line, position in ((1, across), (0, along)):
        block = in_order([block] + [send_plane(block, line, d) for d in (1, 2, 3)], position)
    block = jnp.where(core == 0, jnp.swapaxes(block, 0, 1), block) + 0 * done[0, 0]
    other = send_core(block)
    low, high = jnp.where(core == 0, block, other), jnp.where(core == 0, other, block)
    both = jnp.stack([low, high])
    return both.reshape((EXPERTS,) + both.shape[3:])


def after(value, *done):
    return lax.optimization_barrier((value, done))[0]


def body(
    hidden,
    segments,
    routes,
    attention_gain,
    query_weight,
    key_weight,
    value_weight,
    projection_weight,
    mixture_gain,
    router_weight,
    gate_weight,
    up_weight,
    down_weight,
    cotangent,
):
    me = lax.axis_index("expert")
    mine = lax.axis_index("fsdp")
    core = me % 2
    chip = me // 2
    place_z, place_x = chip // RING, chip % RING
    along = jnp.where(core == 0, place_x, place_z)
    across = jnp.where(core == 0, place_z, place_x)
    same_core = [[2 * i + c for i in range(EXPERTS // 2)] for c in range(2)]

    steps = jnp.arange(16, dtype=jnp.int32)
    from_across, from_along = (across - steps // RING) % RING, (along - steps % RING) % RING
    source_chip = jnp.where(core == 0, from_across * RING + from_along, from_along * RING + from_across)
    at = jnp.concatenate([source_chip, jnp.stack([core, mine, chip])]).astype(jnp.int32)
    here = mine.reshape(1).astype(jnp.int32)

    counts = jnp.stack([jnp.sum(segments < 1), jnp.sum(segments < 2)]).astype(bf16)
    notes = jnp.stack([jnp.concatenate([attention_gain, mixture_gain]), jnp.pad(counts, (0, 510))])
    notes = jnp.pad(notes, ((0, 6), (0, 512)))
    notes = jnp.concatenate([notes, router_weight.T.reshape(4, 8, 256).transpose(1, 0, 2).reshape(8, D)], axis=0)
    head_weights = jnp.concatenate(
        [w.reshape(256, RING, -1) for w in (query_weight, key_weight, value_weight)], axis=2
    ).transpose(1, 0, 2)
    head_weights = jnp.concatenate([head_weights[:, :128], head_weights[:, 128:]], axis=2)

    def message(d):
        return jnp.concatenate([hidden, pick(head_weights, (mine + d) % RING), notes], axis=0)

    messages = [message(0)] + [send_y(message(d), d) for d in (1, 2, 3)]

    named = (routes[:, :, None] == jnp.arange(EXPERTS, dtype=jnp.int32)[None, None, :]).astype(f32).sum(axis=1)
    lower = (jnp.arange(TOK)[:, None] > jnp.arange(TOK)[None, :]).astype(bf16)
    rank = dot(lower, named.astype(bf16))
    slot = jnp.where(named > 0, rank, -1000.0)
    cots = lax.all_gather(cotangent, "expert", axis_index_groups=same_core)

    cosines, sines = rotary_table()
    act, qkv, mixed_heads, mixed_parts, own_w, starts, router = attention_call(
        here, messages, cosines, sines, projection_weight
    )
    down_halves = jnp.concatenate([down_weight[0][:, :512], down_weight[0][:, 512:]], axis=0)
    pack = jnp.concatenate([gate_weight[0], up_weight[0], down_halves], axis=0)
    pack = pack + 0 * starts[0, 0].astype(bf16)
    chip_groups = [[(2 * i + c) * RING + y for c in range(2) for y in range(RING)] for i in range(EXPERTS // 2)]
    packs = lax.all_gather(pack, ("expert", "fsdp"), axis_index_groups=chip_groups).reshape(2, RING, 768, 512)

    mixed_parts = [mixed_parts[0]] + [send_y(mixed_parts[r], -r) for r in (1, 2, 3)]

    gain_two = in_order([part[320:321, 256:512] for part in messages], mine).reshape(D).astype(f32) + 0 * cots[0, 0, 0].astype(f32)


    residual = hidden.astype(f32)
    residual_two = residual + sum(part.astype(f32) for part in mixed_parts)
    scale_two = scale_of(residual_two)
    expert_input = (residual_two * scale_two * gain_two).astype(bf16)

    logits = contract_last(expert_input, router)[:, :EXPERTS]
    logits = jnp.where(named > 0, logits, -1e30)
    gate_weights = jnp.where(named > 0, jnp.exp(logits - jnp.max(logits, axis=1, keepdims=True)), 0.0)
    gate_weights = gate_weights / jnp.sum(gate_weights, axis=1, keepdims=True)
    info = jnp.stack([slot, gate_weights]).transpose(2, 0, 1).reshape(16, 2, 2, TOK).transpose(0, 2, 1, 3)
    info = jnp.pad(info.reshape(16, 4, TOK), ((0, 0), (0, 4), (0, 256 - TOK)), constant_values=-1000.0)
    info = lax.all_to_all(info, "expert", 0, 0, axis_index_groups=same_core, tiled=True)

    x_blocks = gather_plane(expert_input, info)
    orders = [[4, 5, 6, 7, 12, 13, 14, 15], [8, 9, 10, 11, 0, 1, 2, 3]]
    arrivals = [x_blocks[1] + x_blocks[3], x_blocks[2] + x_blocks[0]]
    layouts = [(1, 3, 1, 3), (2, 2, 1, 1, 1, 1)]
    sent, kept = zip(
        *[
            expert_call(orders[i], at, arrivals[i], layouts[i], cots, info, packs)
            for i in range(2)
        ]
    )
    own_grad, other_grad = gradient_call(at, kept)
    returned = scatter_plane(sent[1][2:], sent[0][:2], sent[1][:2], sent[0][2:], own_grad)
    route_delta = returned[:TOK]
    gate_back = returned[TOK:, :512] + returned[TOK:, 512:]
    gate_back = gate_back.reshape(16, 2, 256)[:, :, :TOK].reshape(EXPERTS, TOK).T

    logit_delta = (gate_back - gate_weights * jnp.sum(gate_back, axis=1, keepdims=True)).astype(bf16)
    router_part = contract_rows(expert_input, jnp.pad(logit_delta, ((0, 0), (0, 96))))
    input_delta = route_delta + dot(logit_delta, router[:EXPERTS])
    mixture_part = jnp.sum(input_delta * residual_two * scale_two, axis=0)
    inner = input_delta * gain_two
    upstream = cotangent.astype(f32)
    residual_delta = upstream + scale_two * (
        inner - residual_two * scale_two * scale_two * jnp.mean(inner * residual_two, axis=-1, keepdims=True)
    )
    attention_delta = residual_delta.astype(bf16)

    attention_deltas = [attention_delta] + [send_y(attention_delta, d) for d in (1, 2, 3)]
    weight_part, activation_part, total_grad = attention_back_call(
        here,
        attention_deltas,
        messages,
        [projection_weight, qkv, cosines, sines, mixed_heads, router_part, act, own_w],
        starts,
        mixture_part[None],
        [own_grad, send_core(other_grad)],
    )
    expert_total = lax.psum_scatter(total_grad.reshape(RING * 768, 512), "fsdp", tiled=True)

    produced = produce_call(orders, at, kept, packs, returned)
    produced = lax.all_to_all(produced, "expert", 0, 0, axis_index_groups=same_core, tiled=True)
    wide = ((0, 0), (0, 128 - EXPERTS))
    output = combine_call(
        jnp.pad(slot, wide, constant_values=-1000.0).astype(bf16),
        jnp.pad(gate_weights, wide).astype(bf16),
        residual_two,
        produced,
    )

    activation_parts = [activation_part[0]] + [send_y(activation_part[r], -r) for r in (1, 2, 3)]
    activation_delta = sum(part.astype(f32) for part in activation_parts)
    scale_one = scale_of(residual)
    gain_one = in_order([part[320:321, :256] for part in messages], mine).reshape(D).astype(f32)
    inner = activation_delta * gain_one
    input_gradient = residual_delta + scale_one * (
        inner - residual * scale_one * scale_one * jnp.mean(inner * residual, axis=-1, keepdims=True)
    )

    shared = sum_plane(weight_part, core, along, across)
    held = 0 * sum(part[0, 0].astype(f32) for part in activation_parts[1:] + [produced[0]])
    pieces = (shared[:32].reshape(RING, 8, 640) + held).astype(bf16)
    received = [pick(pieces, mine)] + [send_y(pick(pieces, (mine + d) % RING), d) for d in (1, 2, 3)]
    small = sum(part[:, 512:].astype(f32) for part in received)
    late = in_order([part[:, :512] for part in received], mine)
    shared = jnp.concatenate([late[g] for g in range(RING)] + [shared[32:40, :512], shared[40:, :512], small], axis=1)
    shared = spread_plane(shared.astype(bf16), core, along, across, output).reshape(256, 3200)
    small = shared[:, 3072:].astype(f32)

    expert_total = expert_total.astype(f32)
    gate_gradient = expert_total[None, :256]
    up_gradient = expert_total[None, 256:512]
    down_gradient = jnp.concatenate([expert_total[512:640], expert_total[640:]], axis=1)[None]

    def columns(start, size):
        return jnp.concatenate([shared[:, g * 512 + start : g * 512 + start + size] for g in range(RING)], axis=1)

    query_gradient = columns(0, 256).astype(f32)
    key_gradient = columns(256, 128).astype(f32)
    value_gradient = columns(384, 128).astype(f32)
    projection_gradient = shared[:, 2048:3072].astype(f32)
    return (
        output,
        input_gradient,
        small[:, 33],
        query_gradient,
        key_gradient,
        value_gradient,
        projection_gradient,
        small[:, 32],
        small[:, :32],
        gate_gradient,
        up_gradient,
        down_gradient,
    )


def solution(mesh):
    rows = P(("expert", "fsdp"), None)
    weights = P("fsdp", None)
    experts = P("expert", "fsdp", None)
    return jax.shard_map(
        body,
        mesh=mesh,
        in_specs=(
            rows,
            P(("expert", "fsdp")),
            rows,
            P("fsdp"),
            weights,
            weights,
            weights,
            weights,
            P("fsdp"),
            weights,
            experts,
            experts,
            experts,
            rows,
        ),
        out_specs=(
            rows,
            rows,
            P("fsdp"),
            weights,
            weights,
            weights,
            weights,
            P("fsdp"),
            weights,
            experts,
            experts,
            experts,
        ),
        check_vma=False,
    )
```

```python
import jax
import jax.numpy as jnp
import numpy as np
from jax import lax
from jax.experimental import pallas as pl
from jax.experimental.pallas import tpu as pltpu
from jax.sharding import PartitionSpec as P

D = 1024
HEADS = 16
KV_HEADS = 8
HEAD = 64
FF = 512
TOP = 8
EXPERTS = 32
TOK = 192
CAP = 72
RING = 4
SEQ = RING * TOK
BLOCK = 256
SENT = TOK + 16
WIDE = D + 128
MIB = 1024 * 1024

epsilon = 1e-06
base_theta = 10000.0
bf16 = jnp.bfloat16
f32 = jnp.float32


def place(z, x, core):
    return (z * RING + x) * 2 + core


def plane_perm(line, shift):
    pairs = []
    for z in range(RING):
        for x in range(RING):
            for core in range(2):
                if (core == 0) == (line == 0):
                    to = place(z, (x + shift) % RING, core)
                else:
                    to = place((z + shift) % RING, x, core)
                pairs.append((place(z, x, core), to))
    return pairs


def send_plane(value, line, shift):
    return lax.ppermute(value, "expert", plane_perm(line, shift % RING))


def send_core(value):
    return lax.ppermute(value, "expert", [(i, i ^ 1) for i in range(EXPERTS)])


def send_y(value, shift):
    return lax.ppermute(value, "fsdp", [(i, (i + shift) % RING) for i in range(RING)])


def dot(left, right):
    return jnp.dot(left, right, preferred_element_type=f32)


def contract_rows(left, right):
    return lax.dot_general(left, right, (((0,), (0,)), ((), ())), preferred_element_type=f32)


def contract_last(left, right):
    return lax.dot_general(left, right, (((1,), (1,)), ((), ())), preferred_element_type=f32)


def scale_of(values):
    return lax.rsqrt(jnp.mean(values * values, axis=-1, keepdims=True) + epsilon)


def pick(blocks, index):
    return lax.dynamic_index_in_dim(blocks, index, 0, keepdims=False)


def in_order(received, position):
    own, one, two, three = received
    line = jnp.stack([three, two, one, own, three, two, one])
    return lax.dynamic_slice_in_dim(line, (3 - position) % RING, RING, 0)


def rotary_table():
    frequencies = base_theta ** (-2.0 * np.arange(HEAD // 2, dtype=np.float32) / np.float32(HEAD))
    angles = np.arange(SEQ, dtype=np.float32)[:, None] * frequencies.astype(np.float32)[None, :]
    angles = np.concatenate([angles] * 4, axis=1).astype(np.float32)
    return np.cos(angles).astype(np.float32), np.sin(angles).astype(np.float32)


def at_block(index, size):
    return pl.ds(pl.multiple_of(index * size, size), size)


VMEM = pl.BlockSpec(memory_space=pltpu.VMEM)
SMEM = pl.BlockSpec(memory_space=pltpu.SMEM)
HBM = pl.BlockSpec(memory_space=pltpu.HBM)


class Copies:
    def __init__(self, sems):
        self.sems, self.used = sems, 0

    def start(self, source, target):
        copy = pltpu.make_async_copy(source, target, self.sems.at[self.used])
        self.used += 1
        copy.start()
        return copy


def wait_all(copies):
    for copy in copies:
        copy.wait()


def turn(values, low_half):
    return jnp.where(low_half, -pltpu.roll(values, 96, 1), pltpu.roll(values, 32, 1))


def both_halves(pair):
    low = lax.broadcasted_iota(jnp.int32, pair.shape, 1) < HEAD
    swapped = pltpu.roll(pair, HEAD, 1)
    return jnp.where(low, pair, swapped).astype(bf16), jnp.where(low, swapped, pair).astype(bf16)


def one_half(pair, half):
    low = lax.broadcasted_iota(jnp.int32, pair.shape, 1) < HEAD
    return jnp.where(low == (half == 0), pair, jnp.zeros_like(pair))


def first_visible(place_at, starts):
    return jnp.where(place_at >= starts[1], starts[1], jnp.where(place_at >= starts[0], starts[0], 0))


def attention_kernel(mine, *refs):
    x_refs = refs[:4]
    cos_ref, sin_ref, proj_ref = refs[4:7]
    act_ref, qkv_ref, mixed_ref, part_ref, w_ref, start_ref, router_ref, gain_scr = refs[7:]
    router_ref[...] = jnp.zeros_like(router_ref)
    blocks = [jnp.bitwise_and(mine[0] - r, 3) for r in range(RING)]
    counts = jnp.zeros((1, 128), f32)
    for r in range(RING):
        notes = x_refs[r][TOK + 128 :, :].astype(f32)
        gain_scr[0:1, at_block(blocks[r], 256)] = notes[0:1, :256]
        counts = counts + notes[1:2, :128]
        router = [notes[8:16, 256 * q : 256 * (q + 1)] for q in range(4)]
        router_ref[:EXPERTS, at_block(blocks[r], 256)] = jnp.concatenate(router, axis=0).astype(bf16)
        w_ref[at_block(2 * blocks[r], 128), :] = x_refs[r][TOK : TOK + 128, :512]
        w_ref[at_block(2 * blocks[r] + 1, 128), :] = x_refs[r][TOK : TOK + 128, 512:]
    lanes = lax.broadcasted_iota(jnp.int32, (1, 128), 1)
    starts = [jnp.sum(jnp.where(lanes == i, counts, 0.0), axis=1, keepdims=True).astype(jnp.int32) for i in (0, 1)]
    start_ref[...] = jnp.broadcast_to(jnp.where(lanes == 0, starts[0], starts[1]), (8, 128))
    gain = gain_scr[0:1, :]
    for r in range(RING):
        x = x_refs[r][:TOK, :].astype(f32)
        act_ref[at_block(blocks[r], TOK), :] = (x * scale_of(x) * gain).astype(bf16)
    low = lax.broadcasted_iota(jnp.int32, (BLOCK, 128), 1) % HEAD < HEAD // 2
    for i in range(SEQ // BLOCK):
        span = slice(i * BLOCK, (i + 1) * BLOCK)
        linear = dot(act_ref[span, :], w_ref[...])
        for g in range(3):
            part = linear[:, g * 128 : (g + 1) * 128]
            part = part * cos_ref[span, :] + turn(part, low) * sin_ref[span, :]
            qkv_ref[span, g * 128 : (g + 1) * 128] = part.astype(bf16)
        qkv_ref[span, 384:] = linear[:, 384:].astype(bf16)
    keys = both_halves(qkv_ref[:, 256:384].astype(f32))
    values = both_halves(qkv_ref[:, 384:].astype(f32))
    values = [[one_half(v, h) for h in range(2)] for v in values]
    for i in range(SEQ // BLOCK):
        span, reach = slice(i * BLOCK, (i + 1) * BLOCK), (i + 1) * BLOCK
        query_at = lax.broadcasted_iota(jnp.int32, (BLOCK, 1), 0) + i * BLOCK
        key_at = lax.broadcasted_iota(jnp.int32, (BLOCK, reach), 1)
        visible = jnp.logical_and(key_at <= query_at, key_at >= first_visible(query_at, starts))
        bias = jnp.where(visible, 0.0, -1e30)
        for g in range(2):
            query = qkv_ref[span, g * 128 : (g + 1) * 128]
            total = jnp.zeros((BLOCK, 128), f32)
            for h in range(2):
                scores = contract_last(one_half(query, h), keys[g][:reach]) * HEAD**-0.5 + bias
                exponents = jnp.exp(scores - jnp.max(scores, axis=1, keepdims=True))
                scores = exponents * (1.0 / jnp.sum(exponents, axis=1, keepdims=True))
                total = total + dot(scores.astype(bf16), values[g][h][:reach])
            mixed_ref[span, g * 128 : (g + 1) * 128] = total.astype(bf16)
    for r in range(RING):
        part_ref[r] = dot(mixed_ref[at_block(blocks[r], TOK), :], proj_ref[...]).astype(bf16)


def attention_call(mine, xs, cosines, sines, projection):
    return pl.pallas_call(
        attention_kernel,
        out_shape=[
            jax.ShapeDtypeStruct((SEQ, D), bf16),
            jax.ShapeDtypeStruct((SEQ, 512), bf16),
            jax.ShapeDtypeStruct((SEQ, 256), bf16),
            jax.ShapeDtypeStruct((RING, TOK, D), bf16),
            jax.ShapeDtypeStruct((D, 512), bf16),
            jax.ShapeDtypeStruct((8, 128), jnp.int32),
            jax.ShapeDtypeStruct((128, D), bf16),
        ],
        in_specs=[SMEM] + [VMEM] * 7,
        out_specs=[VMEM] * 7,
        scratch_shapes=[pltpu.VMEM((8, D), f32)],
        compiler_params=pltpu.CompilerParams(vmem_limit_bytes=32 * MIB),
        cost_estimate=pl.CostEstimate(flops=8_000_000_000, bytes_accessed=8_000_000, transcendentals=2_000_000),
    )(mine, *xs, cosines, sines, projection)


def attention_back_kernel(mine, *refs):
    delta_hbm, x_hbm, held_hbm, (start_ref, mixture_ref) = refs[:4], refs[4:8], refs[8:16], refs[16:18]
    (own_hbm, other_hbm, weight_ref, part_ref, grad_ref, delta_scr, x_ref), held = refs[18:25], refs[25:33]
    (md_scr, dq_scr, dk_scr, dv_scr, ld_scr, grad_v, sems) = refs[33:]
    (proj_ref, qkv_ref, cos_ref, sin_ref, mixed_ref, small_ref, act_ref, w_ref) = held
    copies = Copies(sems)
    blocks = [jnp.bitwise_and(mine[0] - r, 3) for r in range(RING)]
    first = [copies.start(delta_hbm[r], delta_scr.at[at_block(blocks[r], TOK)]) for r in range(RING)]
    first += [copies.start(held_hbm[i], held[i]) for i in range(2)]
    later = [copies.start(held_hbm[i], held[i]) for i in range(2, 8)]
    later += [copies.start(x_hbm[r].at[pl.ds(0, TOK)], x_ref.at[r]) for r in range(RING)]
    grads = [copies.start(value, grad_v.at[i]) for i, value in enumerate((own_hbm, other_hbm))]
    wait_all(first)
    md_scr[...] = contract_last(delta_scr[...], proj_ref[...]).astype(bf16)
    starts = [start_ref[0:1, 0:1], start_ref[0:1, 1:2]]
    keys = both_halves(qkv_ref[:, 256:384].astype(f32))
    values = both_halves(qkv_ref[:, 384:].astype(f32))
    scaling = HEAD**-0.5
    dk_scr[...] = jnp.zeros_like(dk_scr)
    dv_scr[...] = jnp.zeros_like(dv_scr)
    for i in range(SEQ // BLOCK):
        span, reach = slice(i * BLOCK, (i + 1) * BLOCK), (i + 1) * BLOCK
        query_at = lax.broadcasted_iota(jnp.int32, (1, BLOCK), 1) + i * BLOCK
        key_at = lax.broadcasted_iota(jnp.int32, (reach, BLOCK), 0)
        visible = jnp.logical_and(key_at <= query_at, key_at >= first_visible(query_at, starts))
        bias = jnp.where(visible, 0.0, -1e30)
        for g in range(2):
            query = qkv_ref[span, g * 128 : (g + 1) * 128]
            delta = md_scr[span, g * 128 : (g + 1) * 128]
            dq = jnp.zeros((BLOCK, 128), f32)
            for h in range(2):
                own_query, own_delta = one_half(query, h), one_half(delta, h)
                scores = contract_last(keys[g][:reach], own_query) * scaling + bias
                exponents = jnp.exp(scores - jnp.max(scores, axis=0, keepdims=True))
                probability = exponents * (1.0 / jnp.sum(exponents, axis=0, keepdims=True))
                probability_delta = contract_last(values[g][:reach], own_delta)
                row_delta = jnp.sum(probability * probability_delta, axis=0, keepdims=True)
                score_delta = (probability * (probability_delta - row_delta)).astype(bf16)
                dk_scr[g, :reach, :] += dot(score_delta, own_query)
                dv_scr[g, :reach, :] += dot(probability.astype(bf16), own_delta)
                dq = dq + contract_rows(score_delta, one_half(keys[g][:reach], h))
            dq_scr[span, g * 128 : (g + 1) * 128] = dq * scaling
    low = lax.broadcasted_iota(jnp.int32, (SEQ, 128), 1) < HEAD
    turned = lax.broadcasted_iota(jnp.int32, (SEQ, 128), 1) % HEAD < HEAD // 2

    def folded(scr):
        first, second = scr[0], scr[1]
        first = first + pltpu.roll(first, HEAD, 1)
        second = second + pltpu.roll(second, HEAD, 1)
        return jnp.where(low, first, second)

    def back(values):
        return values * cos_ref[...] - turn(values * sin_ref[...], turned)

    wait_all(grads)
    for j in range(RING):
        grad_v[0, j] = (grad_v[0, j].astype(f32) + grad_v[1, j].astype(f32)).astype(bf16)
    sent = copies.start(grad_v.at[0], grad_ref)
    wait_all(later)
    for g in range(2):
        ld_scr[:, g * 128 : (g + 1) * 128] = back(dq_scr[:, g * 128 : (g + 1) * 128]).astype(bf16)
    ld_scr[:, 256:384] = back(folded(dk_scr) * scaling).astype(bf16)
    ld_scr[:, 384:] = folded(dv_scr).astype(bf16)
    gain = jnp.zeros((1, D), f32)
    for r in range(RING):
        part = contract_last(ld_scr[at_block(blocks[r], TOK), :], w_ref[...])
        part_ref[r] = part.astype(bf16)
        x = x_ref[r].astype(f32)
        gain = gain + jnp.sum(part * x * scale_of(x), axis=0, keepdims=True)
    lanes = lax.broadcasted_iota(jnp.int32, (256, 128), 1)
    for pair in range(2):
        rows = []
        for j in (2 * pair, 2 * pair + 1):
            span = slice(j * 256, (j + 1) * 256)
            first = jnp.broadcast_to(gain[:, span], (128, 256)).T
            second = jnp.broadcast_to(mixture_ref[:, span], (128, 256)).T
            side = jnp.where(lanes == 33, first, jnp.where(lanes == 32, second, small_ref[span, :]))
            both = jnp.concatenate([contract_rows(act_ref[:, span], ld_scr[...]), side], axis=1)
            rows.append(both.reshape(EXPERTS, 8, 640))
        weight_ref[:, 16 * pair : 16 * pair + 16, :] = jnp.concatenate(rows, axis=1).astype(bf16)
    part = contract_rows(mixed_ref[...], delta_scr[...]).reshape(EXPERTS, 8, D)
    part = jnp.concatenate([part[:, :, :512], part[:, :, 512:]], axis=1).astype(bf16)
    weight_ref[:, 32:, :512] = part
    weight_ref[:, 32:, 512:] = jnp.zeros((EXPERTS, 16, 128), bf16)
    sent.wait()


def attention_back_call(mine, deltas, xs, held, starts, mixture, grads):
    return pl.pallas_call(
        attention_back_kernel,
        out_shape=[
            jax.ShapeDtypeStruct((EXPERTS, 48, 640), bf16),
            jax.ShapeDtypeStruct((RING, TOK, D), bf16),
            jax.ShapeDtypeStruct(grads[0].shape, bf16),
        ],
        in_specs=[SMEM] + [HBM] * 16 + [VMEM] * 2 + [HBM] * 2,
        out_specs=[VMEM] * 2 + [HBM],
        scratch_shapes=[pltpu.VMEM((SEQ, D), bf16), pltpu.VMEM((RING, TOK, D), bf16)]
        + [pltpu.VMEM(value.shape, value.dtype) for value in held]
        + [
            pltpu.VMEM((SEQ, 256), bf16),
            pltpu.VMEM((SEQ, 256), f32),
            pltpu.VMEM((2, SEQ, 128), f32),
            pltpu.VMEM((2, SEQ, 128), f32),
            pltpu.VMEM((SEQ, 512), bf16),
            pltpu.VMEM((2,) + grads[0].shape, bf16),
            pltpu.SemaphoreType.DMA((32,)),
        ],
        compiler_params=pltpu.CompilerParams(vmem_limit_bytes=58 * MIB),
        cost_estimate=pl.CostEstimate(flops=100_000_000, bytes_accessed=100_000, transcendentals=0),
    )(mine, *deltas, *xs, *held, starts, mixture, *grads)


def unpack_kernel(own_ref, other_ref, core, query_ref, key_ref, value_ref, projection_ref, small_ref):
    first = core[0] == 0
    for half in range(2):
        rows = jnp.where(first == (half == 0), own_ref[...], other_ref[...]).astype(f32)
        span = slice(half * 128, (half + 1) * 128)
        for g in range(RING):
            query_ref[span, g * 256 : (g + 1) * 256] = rows[:, g * 512 : g * 512 + 256]
            key_ref[span, g * 128 : (g + 1) * 128] = rows[:, g * 512 + 256 : g * 512 + 384]
            value_ref[span, g * 128 : (g + 1) * 128] = rows[:, g * 512 + 384 : g * 512 + 512]
        projection_ref[span, :] = rows[:, 2048:3072]
        small_ref[span, :] = rows[:, 3072:]


def unpack_call(own, other, core):
    return pl.pallas_call(
        unpack_kernel,
        out_shape=[jax.ShapeDtypeStruct((256, width), f32) for width in (D, 512, 512, D, 128)],
        in_specs=[VMEM, VMEM, SMEM],
        out_specs=[VMEM] * 5,
        compiler_params=pltpu.CompilerParams(vmem_limit_bytes=24 * MIB),
        cost_estimate=pl.CostEstimate(flops=0, bytes_accessed=5_000_000, transcendentals=0),
    )(own, other, core)


def load_gates(copies, packs, e, gate_w, up_w):
    return [
        copies.start(packs.at[e, :, 0:256], gate_w.at[e]),
        copies.start(packs.at[e, :, 256:512], up_w.at[e]),
    ]


def load_down(copies, packs, e, down_w):
    return [
        copies.start(packs.at[e, :, 512:640], down_w.at[e, :, :, 0:512]),
        copies.start(packs.at[e, :, 640:768], down_w.at[e, :, :, 512:1024]),
    ]


def expert_kernel(groups, out_groups, order, at, *refs):
    count, out_count = len(groups), len(out_groups)
    x_refs, refs = refs[:count], refs[count:]
    (cots, info_ref, packs), refs = refs[:3], refs[3:]
    sent_refs, refs = refs[:out_count], refs[out_count:]
    (xs_ref, dy_ref, inner_ref, dg_ref, du_ref), refs = refs[:5], refs[5:]
    (x_v, c_v, info_v, gate_w, up_w, down_w, sent_v, scatter_v), refs = refs[:8], refs[8:]
    (xs_v, dy_v, inner_v, dg_v, du_v, sems) = refs
    chip = at[18]
    copies = Copies(sems)
    sources = [(g, k) for g in range(count) for k in range(groups[g])]
    targets = [(g, k) for g in range(out_count) for k in range(out_groups[g])]
    info_in = copies.start(info_ref, info_v)
    starts = [sum(groups[:g]) for g in range(count)]
    x_in = [copies.start(x_refs[g], x_v.at[pl.ds(starts[g] * TOK, groups[g] * TOK)]) for g in range(count)]
    gates_in, downs_in = [load_gates(copies, packs, 0, gate_w, up_w)], []
    c_in = [copies.start(cots.at[at[order[s]]], c_v.at[s]) for s in range(len(sources))]
    downs_in.append(load_down(copies, packs, 0, down_w))
    gates_in.append(load_gates(copies, packs, 1, gate_w, up_w))
    downs_in.append(load_down(copies, packs, 1, down_w))
    rows = 2 * CAP
    upper = lax.broadcasted_iota(jnp.int32, (rows, 256), 0) < CAP
    pick_at = lax.broadcasted_iota(jnp.int32, (rows, 256), 0)
    pick_at = jnp.where(upper, pick_at, pick_at - CAP).astype(f32)
    tall_at = lax.broadcasted_iota(jnp.int32, (TOK, rows), 1)
    scatter_at = jnp.where(tall_at < CAP, tall_at, tall_at - CAP).astype(f32)
    kind = lax.broadcasted_iota(jnp.int32, (8, rows), 0)
    expert = jnp.where(lax.broadcasted_iota(jnp.int32, (8, rows), 1) < CAP, 0, 1)
    slot_of = (kind == expert).astype(f32).astype(bf16)
    x_parts, dy_parts, picks, weighted = [], [], [], []
    for s in range(len(sources)):
        if s == 0:
            info_in.wait()
        if sources[s][1] == 0:
            x_in[sources[s][0]].wait()
        info = info_v[at[order[s]]]
        pick = jnp.where(upper, info[0:1], info[1:2]) == pick_at
        picks.append(pick.astype(f32))
        chosen = picks[s][:, :TOK].astype(bf16)
        weighted.append(jnp.where(pick, jnp.where(upper, info[2:3], info[3:4]), 0.0)[:, :TOK].astype(bf16))
        info_b = info[:, :TOK].astype(bf16)
        scatter = contract_rows(info_b, slot_of) == scatter_at
        scatter_v[s] = scatter.astype(f32).astype(bf16)
        x_parts.append(dot(chosen, x_v[s * TOK : (s + 1) * TOK, :]))
    out = []
    back, back_gate = [], []
    for e in range(2):
        span = slice(e * CAP, (e + 1) * CAP)
        xs = jnp.concatenate([part[span] for part in x_parts], axis=0).astype(bf16)
        xs_v[e] = xs
        out.append(copies.start(xs_v.at[e], xs_ref.at[e]))
        wait_all(gates_in[e])
        gate_values = dot(xs, gate_w[e].reshape(D, FF))
        up_values = dot(xs, up_w[e].reshape(D, FF))
        if e == 0:
            for s in range(len(sources)):
                c_in[s].wait()
                dy_parts.append(dot(weighted[s], c_v[s]))
        dy = jnp.concatenate([part[span] for part in dy_parts], axis=0).astype(bf16)
        dy_v[e] = dy
        out.append(copies.start(dy_v.at[e], dy_ref.at[e]))
        wait_all(downs_in[e])
        inner_delta = contract_last(dy, down_w[e].reshape(FF, D))
        sigmoid = jax.nn.sigmoid(gate_values)
        silu = gate_values * sigmoid
        inner = silu * up_values
        inner_v[e] = inner.astype(bf16)
        back_gate.append(jnp.sum(inner * inner_delta, axis=1, keepdims=True))
        dg = (inner_delta * up_values * sigmoid * (1.0 + gate_values * (1.0 - sigmoid))).astype(bf16)
        du = (inner_delta * silu).astype(bf16)
        dg_v[e] = dg
        du_v[e] = du
        for value, ref in ((inner_v, inner_ref), (dg_v, dg_ref), (du_v, du_ref)):
            out.append(copies.start(value.at[e], ref.at[e]))
        back.append(contract_last(dg, gate_w[e].reshape(D, FF)) + contract_last(du, up_w[e].reshape(D, FF)))
    row_at = lax.broadcasted_iota(jnp.int32, (16, D), 0)
    for s, (g, k) in enumerate(targets):
        span = slice(s * CAP, (s + 1) * CAP)
        part = jnp.concatenate([back[0][span], back[1][span]], axis=0).astype(bf16)
        sent_v[s, :TOK, :] = dot(scatter_v[s], part).astype(bf16)
        own = [
            jnp.sum(picks[s][e * CAP : (e + 1) * CAP] * back_gate[e][span], axis=0, keepdims=True)
            for e in range(2)
        ]
        high = [value.astype(bf16).astype(f32) for value in own]
        row = jnp.concatenate(high + [own[e] - high[e] for e in range(2)], axis=1)
        sent_v[s, TOK:, :] = jnp.where(row_at == chip, row, 0.0).astype(bf16)
        out.append(copies.start(sent_v.at[s], sent_refs[g].at[pl.ds(k * SENT, SENT)]))
    wait_all(out)


def expert_call(order, at, xs, out_groups, cots, info, packs):
    groups = tuple(x.shape[0] // TOK for x in xs)
    sources = len(order)
    slots = sources * CAP
    count = len(xs)
    kept = [
        ((2, slots, D), bf16),
        ((2, slots, D), bf16),
        ((2, slots, FF), bf16),
        ((2, slots, FF), bf16),
        ((2, slots, FF), bf16),
    ]
    shapes = [jax.ShapeDtypeStruct((g * SENT, D), bf16) for g in out_groups]
    shapes += [jax.ShapeDtypeStruct(*entry) for entry in kept]
    out = pl.pallas_call(
        lambda *refs: expert_kernel(groups, out_groups, order, *refs),
        out_shape=shapes,
        in_specs=[SMEM] + [HBM] * (count + 3),
        out_specs=[HBM] * len(shapes),
        scratch_shapes=[
            pltpu.VMEM((sources * TOK, D), bf16),
            pltpu.VMEM((sources, TOK, D), bf16),
            pltpu.VMEM((16, 8, 256), f32),
            pltpu.VMEM((2, RING, 256, FF), bf16),
            pltpu.VMEM((2, RING, 256, FF), bf16),
            pltpu.VMEM((2, RING, 128, D), bf16),
            pltpu.VMEM((sources, SENT, D), bf16),
            pltpu.VMEM((sources, TOK, 2 * CAP), bf16),
        ]
        + [pltpu.VMEM(*entry) for entry in kept]
        + [pltpu.SemaphoreType.DMA((128,))],
        compiler_params=pltpu.CompilerParams(vmem_limit_bytes=58 * MIB),
        cost_estimate=pl.CostEstimate(
            flops=2 * 2 * slots * D * FF * 16, bytes_accessed=26_000_000, transcendentals=2 * slots * FF
        ),
    )(at, *xs, cots, info, packs)
    return out[: len(out_groups)], out[len(out_groups) :]


def produce_kernel(orders, at, *refs):
    count = len(orders)
    inner_refs, (packs, _, out_ref, inner_v, down_w, out_v, sems) = refs[:count], refs[count:]
    copies = Copies(sems)
    downs_in = load_down(copies, packs, 0, down_w) + load_down(copies, packs, 1, down_w)
    ins = [copies.start(inner_refs[i], inner_v.at[:, pl.ds(8 * i * CAP, 8 * CAP)]) for i in range(count)]
    wait_all(downs_in)
    outs = []
    for i, order in enumerate(orders):
        ins[i].wait()
        rows = slice(8 * i * CAP, 8 * (i + 1) * CAP)
        produced = [dot(inner_v[e, rows, :], down_w[e].reshape(FF, D)) for e in range(2)]
        for s, source in enumerate(order):
            span = slice(s * CAP, (s + 1) * CAP)
            out_v[source] = jnp.concatenate([produced[0][span], produced[1][span]], axis=0).astype(bf16)
            outs.append(copies.start(out_v.at[source], out_ref.at[at[source]]))
    wait_all(outs)


def produce_call(orders, at, kept, packs, done):
    inners = [chunk[2] for chunk in kept]
    return pl.pallas_call(
        lambda *refs: produce_kernel(orders, *refs),
        out_shape=jax.ShapeDtypeStruct((16, 2 * CAP, D), bf16),
        in_specs=[SMEM] + [HBM] * (len(orders) + 2),
        out_specs=HBM,
        scratch_shapes=[
            pltpu.VMEM((2, 16 * CAP, FF), bf16),
            pltpu.VMEM((2, RING, 128, D), bf16),
            pltpu.VMEM((16, 2 * CAP, D), bf16),
            pltpu.SemaphoreType.DMA((64,)),
        ],
        compiler_params=pltpu.CompilerParams(vmem_limit_bytes=58 * MIB),
        cost_estimate=pl.CostEstimate(
            flops=2 * 2 * 1152 * D * FF * 3, bytes_accessed=14_000_000, transcendentals=0
        ),
    )(at, *inners, packs, done)


def combine_kernel(slot_ref, gate_ref, residual_ref, rows_ref, out_ref, rows_v, sems):
    copies = Copies(sems)
    ins = [copies.start(rows_ref.at[p], rows_v.at[p]) for p in range(16)]
    lane = lax.broadcasted_iota(jnp.int32, (TOK, 2 * CAP), 1)
    slot_at = jnp.where(lane < CAP, lane, lane - CAP).astype(f32)
    at_row = lax.broadcasted_iota(jnp.int32, (128, 2 * CAP), 0)
    at_half = jnp.where(lax.broadcasted_iota(jnp.int32, (128, 2 * CAP), 1) < CAP, 0, 1)
    total = residual_ref[...]
    for p in range(16):
        own = (at_row == 2 * p + at_half).astype(f32).astype(bf16)
        here = dot(slot_ref[...], own) == slot_at
        weight = jnp.where(here, dot(gate_ref[...], own), 0.0).astype(bf16)
        ins[p].wait()
        total = total + dot(weight, rows_v[p])
    out_ref[...] = total.astype(bf16)


def combine_call(slots, gates, residual, rows):
    return pl.pallas_call(
        combine_kernel,
        out_shape=jax.ShapeDtypeStruct((TOK, D), bf16),
        in_specs=[VMEM] * 3 + [HBM],
        out_specs=VMEM,
        scratch_shapes=[pltpu.VMEM((16, 2 * CAP, D), bf16), pltpu.SemaphoreType.DMA((16,))],
        compiler_params=pltpu.CompilerParams(vmem_limit_bytes=24 * MIB),
        cost_estimate=pl.CostEstimate(flops=2_000_000_000, bytes_accessed=6_000_000, transcendentals=0),
    )(slots, gates, residual, rows)


def gradient_kernel(at, *refs):
    chunks = [refs[5 * i : 5 * i + 5] for i in range((len(refs) - 8) // 5)]
    own_ref, other_ref, xs_v, dy_v, inner_v, both_v, out_v, sems = refs[-8:]
    core = at[16]
    copies = Copies(sems)
    gate_in, down_in, start = [], [], 0
    for xs, dy, inner, dg, du in chunks:
        span = pl.ds(start, xs.shape[1])
        start += xs.shape[1]
        gate_in.append(copies.start(xs, xs_v.at[:, span]))
        gate_in.append(copies.start(dg, both_v.at[:, span, 0:FF]))
        gate_in.append(copies.start(du, both_v.at[:, span, FF : 2 * FF]))
        down_in.append(copies.start(inner, inner_v.at[:, span]))
        down_in.append(copies.start(dy, dy_v.at[:, span]))
    outs = []
    for e in range(2):
        if e == 0:
            wait_all(gate_in)
        for j in range(RING):
            part = contract_rows(xs_v[e, :, j * 256 : (j + 1) * 256], both_v[e]).astype(bf16)
            out_v[e, j, 0:256, :] = part[:, :FF]
            out_v[e, j, 256:512, :] = part[:, FF:]
        if e == 0:
            wait_all(down_in)
        for j in range(RING):
            part = contract_rows(inner_v[e, :, j * 128 : (j + 1) * 128], dy_v[e]).astype(bf16)
            out_v[e, j, 512:640, :] = part[:, :512]
            out_v[e, j, 640:768, :] = part[:, 512:]
    outs.append(copies.start(out_v.at[1 - core], other_ref))
    outs.append(copies.start(out_v.at[core], own_ref))
    wait_all(outs)


def gradient_call(at, kept):
    size = sum(chunk[0].shape[1] for chunk in kept)
    operands = [entry for chunk in kept for entry in chunk]
    return pl.pallas_call(
        gradient_kernel,
        out_shape=[jax.ShapeDtypeStruct((RING, 768, 512), bf16)] * 2,
        in_specs=[SMEM] + [HBM] * len(operands),
        out_specs=[HBM] * 2,
        scratch_shapes=[
            pltpu.VMEM((2, size, D), bf16),
            pltpu.VMEM((2, size, D), bf16),
            pltpu.VMEM((2, size, FF), bf16),
            pltpu.VMEM((2, size, 2 * FF), bf16),
            pltpu.VMEM((2, RING, 768, 512), bf16),
            pltpu.SemaphoreType.DMA((64,)),
        ],
        compiler_params=pltpu.CompilerParams(vmem_limit_bytes=58 * MIB),
        cost_estimate=pl.CostEstimate(
            flops=2 * 2 * 1152 * D * FF * 6, bytes_accessed=24_000_000, transcendentals=0
        ),
    )(at, *operands)


def gather_plane(own, info):
    near = [send_plane(own, 0, d) for d in (1, 2, 3)]
    own_one, own_three = send_plane(own, 1, 1), send_plane(own, 1, 3)
    rest = jnp.concatenate(near, axis=0)
    rest_one, rest_three = send_plane(rest, 1, 1), send_plane(rest, 1, 3)
    own_two = send_plane(own_one, 1, 1)
    held = 0 * info[0, 0, 0].astype(bf16)
    low_two = send_plane(rest_one[:TOK] + held, 1, 1)
    high_two = send_plane(rest_three[TOK:] + held, 1, 3)
    return [own] + near, [own_one, rest_one], [own_two, low_two, high_two], [own_three, rest_three]


def add(left, right):
    return (left.astype(f32) + right.astype(f32)).astype(bf16)


def scatter_far(one, two, three):
    low = send_plane(two[0], 1, 3)
    high = send_plane(two[1], 1, 1)
    rest_three = jnp.concatenate([three[1][:SENT], add(three[1][SENT:], high)], axis=0)
    rest_one = jnp.concatenate([add(one[1][:SENT], low[SENT:]), one[1][SENT:]], axis=0)
    return add(one[0], low[:SENT]), rest_one, three[0], rest_three


def scatter_near(own, parts, before):
    before = 0 * before[0, 0, 0].astype(f32)
    own_one, rest_one = (send_plane(part, 1, 3) for part in parts[:2])
    own_three, rest_three = (send_plane(part, 1, 1) for part in parts[2:])
    total = own[0].astype(f32) + own_one.astype(f32) + own_three.astype(f32)
    for d in (1, 2, 3):
        span = slice((d - 1) * SENT, d * SENT)
        part = own[d].astype(f32) + before + rest_one[span].astype(f32) + rest_three[span].astype(f32)
        total = total + send_plane(part.astype(bf16), 0, -d).astype(f32)
    return total, rest_one


def sum_plane(blocks, core, along, across):
    blocks = blocks.reshape((2, RING, RING) + blocks.shape[1:])
    blocks = add(pick(blocks, core), send_core(pick(blocks, 1 - core)))
    for line, position in ((0, along), (1, across)):
        parts = [pick(blocks, position)]
        parts += [send_plane(pick(blocks, (position + d) % RING), line, d) for d in (1, 2, 3)]
        total = sum(part.astype(f32) for part in parts)
        blocks = total.astype(bf16)
    return total


def spread_plane(block, along, across, done):
    for line, position in ((1, across), (0, along)):
        block = in_order([block] + [send_plane(block, line, d) for d in (1, 2, 3)], position)
    block = block.reshape(128, block.shape[-1]) + 0 * done
    return block, send_core(block)


def body(
    hidden,
    segments,
    routes,
    attention_gain,
    query_weight,
    key_weight,
    value_weight,
    projection_weight,
    mixture_gain,
    router_weight,
    gate_weight,
    up_weight,
    down_weight,
    cotangent,
):
    me = lax.axis_index("expert")
    mine = lax.axis_index("fsdp")
    core = me % 2
    chip = me // 2
    place_z, place_x = chip // RING, chip % RING
    along = jnp.where(core == 0, place_x, place_z)
    across = jnp.where(core == 0, place_z, place_x)
    same_core = [[2 * i + c for i in range(EXPERTS // 2)] for c in range(2)]

    steps = jnp.arange(16, dtype=jnp.int32)
    from_across, from_along = (across - steps // RING) % RING, (along - steps % RING) % RING
    source_chip = jnp.where(core == 0, from_across * RING + from_along, from_along * RING + from_across)
    at = jnp.concatenate([source_chip, jnp.stack([core, mine, chip])]).astype(jnp.int32)
    here = mine.reshape(1).astype(jnp.int32)

    counts = jnp.stack([jnp.sum(segments < 1), jnp.sum(segments < 2)]).astype(bf16)
    notes = jnp.stack([jnp.concatenate([attention_gain, mixture_gain]), jnp.pad(counts, (0, 510))])
    notes = jnp.pad(notes, ((0, 6), (0, 512)))
    notes = jnp.concatenate([notes, router_weight.T.reshape(4, 8, 256).transpose(1, 0, 2).reshape(8, D)], axis=0)
    head_weights = jnp.concatenate(
        [w.reshape(256, RING, -1) for w in (query_weight, key_weight, value_weight)], axis=2
    ).transpose(1, 0, 2)
    head_weights = jnp.concatenate([head_weights[:, :128], head_weights[:, 128:]], axis=2)

    def message(d):
        return jnp.concatenate([hidden, pick(head_weights, (mine + d) % RING), notes], axis=0)

    messages = [message(0)] + [send_y(message(d), d) for d in (1, 2, 3)]

    named = (routes[:, :, None] == jnp.arange(EXPERTS, dtype=jnp.int32)[None, None, :]).astype(f32).sum(axis=1)
    lower = (jnp.arange(TOK)[:, None] > jnp.arange(TOK)[None, :]).astype(bf16)
    rank = dot(lower, named.astype(bf16))
    slot = jnp.where(named > 0, rank, -1000.0)
    cots = lax.all_gather(cotangent, "expert", axis_index_groups=same_core)

    cosines, sines = rotary_table()
    act, qkv, mixed_heads, mixed_parts, own_w, starts, router = attention_call(
        here, messages, cosines, sines, projection_weight
    )

    mixed_parts = [mixed_parts[0]] + [send_y(mixed_parts[r], -r) for r in (1, 2, 3)]

    gain_two = in_order([part[320:321, 256:512] for part in messages], mine).reshape(D).astype(f32)


    residual = hidden.astype(f32)
    residual_two = residual + sum(part.astype(f32) for part in mixed_parts)
    scale_two = scale_of(residual_two)
    expert_input = (residual_two * scale_two * gain_two).astype(bf16)

    down_halves = jnp.concatenate([down_weight[0][:, :512], down_weight[0][:, 512:]], axis=0)
    pack = jnp.concatenate([gate_weight[0], up_weight[0], down_halves], axis=0)
    pack = pack + 0 * scale_two[0, 0].astype(bf16)
    chip_groups = [[(2 * i + c) * RING + y for c in range(2) for y in range(RING)] for i in range(EXPERTS // 2)]
    packs = lax.all_gather(pack, ("expert", "fsdp"), axis_index_groups=chip_groups).reshape(2, RING, 768, 512)

    logits = contract_last(expert_input, router)[:, :EXPERTS]
    logits = jnp.where(named > 0, logits, -1e30)
    gate_weights = jnp.where(named > 0, jnp.exp(logits - jnp.max(logits, axis=1, keepdims=True)), 0.0)
    gate_weights = gate_weights / jnp.sum(gate_weights, axis=1, keepdims=True)
    info = jnp.stack([slot, gate_weights + 0 * cots[0, 0, 0].astype(f32)]).transpose(2, 0, 1).reshape(16, 2, 2, TOK).transpose(0, 2, 1, 3)
    info = jnp.pad(info.reshape(16, 4, TOK), ((0, 0), (0, 4), (0, 256 - TOK)), constant_values=-1000.0)
    info = lax.all_to_all(info, "expert", 0, 0, axis_index_groups=same_core, tiled=True)

    x_blocks = gather_plane(expert_input, info)
    orders = [[4, 5, 6, 7, 12, 13, 14, 15], [8, 9, 10, 11, 0, 1, 2, 3]]
    arrivals = [x_blocks[1] + x_blocks[3], x_blocks[2] + x_blocks[0]]
    layouts = [(1, 3, 1, 3), (2, 2, 1, 1, 1, 1)]
    sent, kept = zip(
        *[
            expert_call(orders[i], at, arrivals[i], layouts[i], cots, info, packs)
            for i in range(2)
        ]
    )
    near_parts = scatter_far(sent[0][:2], sent[1][:2], sent[0][2:])
    own_grad, other_grad = gradient_call(at, kept)
    returned, arrived = scatter_near(sent[1][2:], near_parts, own_grad)
    route_delta = returned[:TOK]
    gate_back = returned[TOK:, :512] + returned[TOK:, 512:]
    gate_back = gate_back.reshape(16, 2, 256)[:, :, :TOK].reshape(EXPERTS, TOK).T

    logit_delta = (gate_back - gate_weights * jnp.sum(gate_back, axis=1, keepdims=True)).astype(bf16)
    router_part = contract_rows(expert_input, jnp.pad(logit_delta, ((0, 0), (0, 96))))
    input_delta = route_delta + dot(logit_delta, router[:EXPERTS])
    mixture_part = jnp.sum(input_delta * residual_two * scale_two, axis=0)
    inner = input_delta * gain_two
    upstream = cotangent.astype(f32)
    residual_delta = upstream + scale_two * (
        inner - residual_two * scale_two * scale_two * jnp.mean(inner * residual_two, axis=-1, keepdims=True)
    )
    attention_delta = residual_delta.astype(bf16)

    attention_deltas = [attention_delta] + [send_y(attention_delta, d) for d in (1, 2, 3)]
    weight_part, activation_part, total_grad = attention_back_call(
        here,
        attention_deltas,
        messages,
        [projection_weight, qkv, cosines, sines, mixed_heads, router_part, act, own_w],
        starts,
        mixture_part[None],
        [own_grad, send_core(other_grad)],
    )
    expert_total = lax.psum_scatter(total_grad.reshape(RING * 768, 512), "fsdp", tiled=True)

    produced = produce_call(orders, at, kept, packs, arrived)
    produced = lax.all_to_all(produced, "expert", 0, 0, axis_index_groups=same_core, tiled=True)
    wide = ((0, 0), (0, 128 - EXPERTS))
    output = combine_call(
        jnp.pad(slot, wide, constant_values=-1000.0).astype(bf16),
        jnp.pad(gate_weights, wide).astype(bf16),
        residual_two,
        produced,
    )

    activation_parts = [activation_part[0]] + [send_y(activation_part[r], -r) for r in (1, 2, 3)]
    activation_delta = sum(part.astype(f32) for part in activation_parts)
    scale_one = scale_of(residual)
    gain_one = in_order([part[320:321, :256] for part in messages], mine).reshape(D).astype(f32)
    inner = activation_delta * gain_one
    input_gradient = residual_delta + scale_one * (
        inner - residual * scale_one * scale_one * jnp.mean(inner * residual, axis=-1, keepdims=True)
    )

    shared = sum_plane(weight_part, core, along, across)
    held = 0 * (activation_delta[0, 0] + produced[0, 0, 0].astype(f32))
    pieces = (shared[:32].reshape(RING, 8, 640) + held).astype(bf16)
    received = [pick(pieces, mine)] + [send_y(pick(pieces, (mine + d) % RING), d) for d in (1, 2, 3)]
    small = sum(part[:, 512:].astype(f32) for part in received) + 0 * output[0, 0].astype(f32)
    late = in_order([part[:, :512] for part in received], mine)
    shared = jnp.concatenate([late[g] for g in range(RING)] + [shared[32:40, :512], shared[40:, :512], small], axis=1)
    own, other = spread_plane(shared.astype(bf16), along, across, expert_total[0, 0])
    query_gradient, key_gradient, value_gradient, projection_gradient, small = unpack_call(
        own, other, core.reshape(1).astype(jnp.int32)
    )

    expert_total = expert_total.astype(f32)
    gate_gradient = expert_total[None, :256]
    up_gradient = expert_total[None, 256:512]
    down_gradient = jnp.concatenate([expert_total[512:640], expert_total[640:]], axis=1)[None]

    return (
        output,
        input_gradient,
        small[:, 33],
        query_gradient,
        key_gradient,
        value_gradient,
        projection_gradient,
        small[:, 32],
        small[:, :32],
        gate_gradient,
        up_gradient,
        down_gradient,
    )


def solution(mesh):
    rows = P(("expert", "fsdp"), None)
    weights = P("fsdp", None)
    experts = P("expert", "fsdp", None)
    return jax.shard_map(
        body,
        mesh=mesh,
        in_specs=(
            rows,
            P(("expert", "fsdp")),
            rows,
            P("fsdp"),
            weights,
            weights,
            weights,
            weights,
            P("fsdp"),
            weights,
            experts,
            experts,
            experts,
            rows,
        ),
        out_specs=(
            rows,
            rows,
            P("fsdp"),
            weights,
            weights,
            weights,
            weights,
            P("fsdp"),
            weights,
            experts,
            experts,
            experts,
        ),
        check_vma=False,
    )
```

```python
import jax
import jax.numpy as jnp
import numpy as np
from jax import lax
from jax.experimental import pallas as pl
from jax.experimental.pallas import tpu as pltpu
from jax.sharding import PartitionSpec as P

D = 1024
HEADS = 16
KV_HEADS = 8
HEAD = 64
FF = 512
TOP = 8
EXPERTS = 32
TOK = 192
CAP = 72
RING = 4
SEQ = RING * TOK
BLOCK = 256
SENT = TOK + 16
WIDE = D + 128
MIB = 1024 * 1024

epsilon = 1e-06
base_theta = 10000.0
bf16 = jnp.bfloat16
f32 = jnp.float32


def place(z, x, core):
    return (z * RING + x) * 2 + core


def plane_perm(line, shift):
    pairs = []
    for z in range(RING):
        for x in range(RING):
            for core in range(2):
                if (core == 0) == (line == 0):
                    to = place(z, (x + shift) % RING, core)
                else:
                    to = place((z + shift) % RING, x, core)
                pairs.append((place(z, x, core), to))
    return pairs


def send_plane(value, line, shift):
    return lax.ppermute(value, "expert", plane_perm(line, shift % RING))


def send_core(value):
    return lax.ppermute(value, "expert", [(i, i ^ 1) for i in range(EXPERTS)])


def send_y(value, shift):
    return lax.ppermute(value, "fsdp", [(i, (i + shift) % RING) for i in range(RING)])


def dot(left, right):
    return jnp.dot(left, right, preferred_element_type=f32)


def contract_rows(left, right):
    return lax.dot_general(left, right, (((0,), (0,)), ((), ())), preferred_element_type=f32)


def contract_last(left, right):
    return lax.dot_general(left, right, (((1,), (1,)), ((), ())), preferred_element_type=f32)


def scale_of(values):
    return lax.rsqrt(jnp.mean(values * values, axis=-1, keepdims=True) + epsilon)


def pick(blocks, index):
    return lax.dynamic_index_in_dim(blocks, index, 0, keepdims=False)


def in_order(received, position):
    own, one, two, three = received
    line = jnp.stack([three, two, one, own, three, two, one])
    return lax.dynamic_slice_in_dim(line, (3 - position) % RING, RING, 0)


def rotary_table():
    frequencies = base_theta ** (-2.0 * np.arange(HEAD // 2, dtype=np.float32) / np.float32(HEAD))
    angles = np.arange(SEQ, dtype=np.float32)[:, None] * frequencies.astype(np.float32)[None, :]
    angles = np.concatenate([angles] * 4, axis=1).astype(np.float32)
    return np.cos(angles).astype(np.float32), np.sin(angles).astype(np.float32)


def at_block(index, size):
    return pl.ds(pl.multiple_of(index * size, size), size)


VMEM = pl.BlockSpec(memory_space=pltpu.VMEM)
SMEM = pl.BlockSpec(memory_space=pltpu.SMEM)
HBM = pl.BlockSpec(memory_space=pltpu.HBM)


class Copies:
    def __init__(self, sems):
        self.sems, self.used = sems, 0

    def start(self, source, target):
        copy = pltpu.make_async_copy(source, target, self.sems.at[self.used])
        self.used += 1
        copy.start()
        return copy


def wait_all(copies):
    for copy in copies:
        copy.wait()


def turn(values, low_half):
    return jnp.where(low_half, -pltpu.roll(values, 96, 1), pltpu.roll(values, 32, 1))


def both_halves(pair):
    low = lax.broadcasted_iota(jnp.int32, pair.shape, 1) < HEAD
    swapped = pltpu.roll(pair, HEAD, 1)
    return jnp.where(low, pair, swapped).astype(bf16), jnp.where(low, swapped, pair).astype(bf16)


def one_half(pair, half):
    low = lax.broadcasted_iota(jnp.int32, pair.shape, 1) < HEAD
    return jnp.where(low == (half == 0), pair, jnp.zeros_like(pair))


def first_visible(place_at, starts):
    return jnp.where(place_at >= starts[1], starts[1], jnp.where(place_at >= starts[0], starts[0], 0))


def attention_kernel(mine, *refs):
    x_refs = refs[:4]
    cos_ref, sin_ref, proj_ref = refs[4:7]
    act_ref, qkv_ref, mixed_ref, part_ref, w_ref, start_ref, router_ref, gain_scr = refs[7:]
    router_ref[...] = jnp.zeros_like(router_ref)
    blocks = [jnp.bitwise_and(mine[0] - r, 3) for r in range(RING)]
    counts = jnp.zeros((1, 128), f32)
    for r in range(RING):
        notes = x_refs[r][TOK + 128 :, :].astype(f32)
        gain_scr[0:1, at_block(blocks[r], 256)] = notes[0:1, :256]
        counts = counts + notes[1:2, :128]
        router = [notes[8:16, 256 * q : 256 * (q + 1)] for q in range(4)]
        router_ref[:EXPERTS, at_block(blocks[r], 256)] = jnp.concatenate(router, axis=0).astype(bf16)
        w_ref[at_block(2 * blocks[r], 128), :] = x_refs[r][TOK : TOK + 128, :512]
        w_ref[at_block(2 * blocks[r] + 1, 128), :] = x_refs[r][TOK : TOK + 128, 512:]
    lanes = lax.broadcasted_iota(jnp.int32, (1, 128), 1)
    starts = [jnp.sum(jnp.where(lanes == i, counts, 0.0), axis=1, keepdims=True).astype(jnp.int32) for i in (0, 1)]
    start_ref[...] = jnp.broadcast_to(jnp.where(lanes == 0, starts[0], starts[1]), (8, 128))
    gain = gain_scr[0:1, :]
    for r in range(RING):
        x = x_refs[r][:TOK, :].astype(f32)
        act_ref[at_block(blocks[r], TOK), :] = (x * scale_of(x) * gain).astype(bf16)
    low = lax.broadcasted_iota(jnp.int32, (BLOCK, 128), 1) % HEAD < HEAD // 2
    for i in range(SEQ // BLOCK):
        span = slice(i * BLOCK, (i + 1) * BLOCK)
        linear = dot(act_ref[span, :], w_ref[...])
        for g in range(3):
            part = linear[:, g * 128 : (g + 1) * 128]
            part = part * cos_ref[span, :] + turn(part, low) * sin_ref[span, :]
            qkv_ref[span, g * 128 : (g + 1) * 128] = part.astype(bf16)
        qkv_ref[span, 384:] = linear[:, 384:].astype(bf16)
    keys = both_halves(qkv_ref[:, 256:384].astype(f32))
    values = both_halves(qkv_ref[:, 384:].astype(f32))
    values = [[one_half(v, h) for h in range(2)] for v in values]
    for i in range(SEQ // BLOCK):
        span, reach = slice(i * BLOCK, (i + 1) * BLOCK), (i + 1) * BLOCK
        query_at = lax.broadcasted_iota(jnp.int32, (BLOCK, 1), 0) + i * BLOCK
        key_at = lax.broadcasted_iota(jnp.int32, (BLOCK, reach), 1)
        visible = jnp.logical_and(key_at <= query_at, key_at >= first_visible(query_at, starts))
        bias = jnp.where(visible, 0.0, -1e30)
        for g in range(2):
            query = qkv_ref[span, g * 128 : (g + 1) * 128]
            total = jnp.zeros((BLOCK, 128), f32)
            for h in range(2):
                scores = contract_last(one_half(query, h), keys[g][:reach]) * HEAD**-0.5 + bias
                exponents = jnp.exp(scores - jnp.max(scores, axis=1, keepdims=True))
                scores = exponents * (1.0 / jnp.sum(exponents, axis=1, keepdims=True))
                total = total + dot(scores.astype(bf16), values[g][h][:reach])
            mixed_ref[span, g * 128 : (g + 1) * 128] = total.astype(bf16)
    for r in range(RING):
        part_ref[r] = dot(mixed_ref[at_block(blocks[r], TOK), :], proj_ref[...]).astype(bf16)


def attention_call(mine, xs, cosines, sines, projection):
    return pl.pallas_call(
        attention_kernel,
        out_shape=[
            jax.ShapeDtypeStruct((SEQ, D), bf16),
            jax.ShapeDtypeStruct((SEQ, 512), bf16),
            jax.ShapeDtypeStruct((SEQ, 256), bf16),
            jax.ShapeDtypeStruct((RING, TOK, D), bf16),
            jax.ShapeDtypeStruct((D, 512), bf16),
            jax.ShapeDtypeStruct((8, 128), jnp.int32),
            jax.ShapeDtypeStruct((128, D), bf16),
        ],
        in_specs=[SMEM] + [VMEM] * 7,
        out_specs=[VMEM] * 7,
        scratch_shapes=[pltpu.VMEM((8, D), f32)],
        compiler_params=pltpu.CompilerParams(vmem_limit_bytes=32 * MIB),
        cost_estimate=pl.CostEstimate(flops=8_000_000_000, bytes_accessed=8_000_000, transcendentals=2_000_000),
    )(mine, *xs, cosines, sines, projection)


def attention_back_kernel(mine, *refs):
    delta_hbm, x_hbm, held_hbm, (start_ref, mixture_ref) = refs[:4], refs[4:8], refs[8:16], refs[16:18]
    (own_hbm, other_hbm, weight_ref, part_ref, grad_ref, delta_scr, x_ref), held = refs[18:25], refs[25:33]
    (md_scr, dq_scr, dk_scr, dv_scr, ld_scr, grad_v, sems) = refs[33:]
    (proj_ref, qkv_ref, cos_ref, sin_ref, mixed_ref, small_ref, act_ref, w_ref) = held
    copies = Copies(sems)
    blocks = [jnp.bitwise_and(mine[0] - r, 3) for r in range(RING)]
    first = [copies.start(delta_hbm[r], delta_scr.at[at_block(blocks[r], TOK)]) for r in range(RING)]
    first += [copies.start(held_hbm[i], held[i]) for i in range(2)]
    later = [copies.start(held_hbm[i], held[i]) for i in range(2, 8)]
    later += [copies.start(x_hbm[r].at[pl.ds(0, TOK)], x_ref.at[r]) for r in range(RING)]
    grads = [copies.start(value, grad_v.at[i]) for i, value in enumerate((own_hbm, other_hbm))]
    wait_all(first)
    md_scr[...] = contract_last(delta_scr[...], proj_ref[...]).astype(bf16)
    starts = [start_ref[0:1, 0:1], start_ref[0:1, 1:2]]
    keys = both_halves(qkv_ref[:, 256:384].astype(f32))
    values = both_halves(qkv_ref[:, 384:].astype(f32))
    halves = [[one_half(k, h) for h in range(2)] for k in keys]
    scaling = HEAD**-0.5
    dk_scr[...] = jnp.zeros_like(dk_scr)
    dv_scr[...] = jnp.zeros_like(dv_scr)
    for i in range(SEQ // BLOCK):
        span, reach = slice(i * BLOCK, (i + 1) * BLOCK), (i + 1) * BLOCK
        query_at = lax.broadcasted_iota(jnp.int32, (1, BLOCK), 1) + i * BLOCK
        key_at = lax.broadcasted_iota(jnp.int32, (reach, BLOCK), 0)
        visible = jnp.logical_and(key_at <= query_at, key_at >= first_visible(query_at, starts))
        bias = jnp.where(visible, 0.0, -1e30)
        for g in range(2):
            query = qkv_ref[span, g * 128 : (g + 1) * 128]
            delta = md_scr[span, g * 128 : (g + 1) * 128]
            dq = jnp.zeros((128, BLOCK), f32)
            for h in range(2):
                own_query, own_delta = one_half(query, h), one_half(delta, h)
                scores = contract_last(keys[g][:reach], own_query) * scaling + bias
                exponents = jnp.exp(scores - jnp.max(scores, axis=0, keepdims=True))
                probability = exponents * (1.0 / jnp.sum(exponents, axis=0, keepdims=True))
                probability_delta = contract_last(values[g][:reach], own_delta)
                row_delta = jnp.sum(probability * probability_delta, axis=0, keepdims=True)
                score_delta = (probability * (probability_delta - row_delta)).astype(bf16)
                dk_scr[g, :reach, :] += dot(score_delta, own_query)
                dv_scr[g, :reach, :] += dot(probability.astype(bf16), own_delta)
                dq = dq + contract_rows(halves[g][h][:reach], score_delta)
            dq_scr[span, g * 128 : (g + 1) * 128] = dq.T * scaling
    low = lax.broadcasted_iota(jnp.int32, (SEQ, 128), 1) < HEAD
    turned = lax.broadcasted_iota(jnp.int32, (SEQ, 128), 1) % HEAD < HEAD // 2

    def folded(scr):
        first, second = scr[0], scr[1]
        first = first + pltpu.roll(first, HEAD, 1)
        second = second + pltpu.roll(second, HEAD, 1)
        return jnp.where(low, first, second)

    def back(values):
        return values * cos_ref[...] - turn(values * sin_ref[...], turned)

    wait_all(grads)
    for j in range(RING):
        grad_v[0, j] = (grad_v[0, j].astype(f32) + grad_v[1, j].astype(f32)).astype(bf16)
    sent = copies.start(grad_v.at[0], grad_ref)
    wait_all(later)
    for g in range(2):
        ld_scr[:, g * 128 : (g + 1) * 128] = back(dq_scr[:, g * 128 : (g + 1) * 128]).astype(bf16)
    ld_scr[:, 256:384] = back(folded(dk_scr) * scaling).astype(bf16)
    ld_scr[:, 384:] = folded(dv_scr).astype(bf16)
    gain = jnp.zeros((1, D), f32)
    for r in range(RING):
        part = contract_last(ld_scr[at_block(blocks[r], TOK), :], w_ref[...])
        part_ref[r] = part.astype(bf16)
        x = x_ref[r].astype(f32)
        gain = gain + jnp.sum(part * x * scale_of(x), axis=0, keepdims=True)
    lanes = lax.broadcasted_iota(jnp.int32, (256, 128), 1)
    for pair in range(2):
        rows = []
        for j in (2 * pair, 2 * pair + 1):
            span = slice(j * 256, (j + 1) * 256)
            first = jnp.broadcast_to(gain[:, span], (128, 256)).T
            second = jnp.broadcast_to(mixture_ref[:, span], (128, 256)).T
            side = jnp.where(lanes == 33, first, jnp.where(lanes == 32, second, small_ref[span, :]))
            both = jnp.concatenate([contract_rows(act_ref[:, span], ld_scr[...]), side], axis=1)
            rows.append(both.reshape(EXPERTS, 8, 640))
        weight_ref[:, 16 * pair : 16 * pair + 16, :] = jnp.concatenate(rows, axis=1).astype(bf16)
    part = contract_rows(mixed_ref[...], delta_scr[...]).reshape(EXPERTS, 8, D)
    part = jnp.concatenate([part[:, :, :512], part[:, :, 512:]], axis=1).astype(bf16)
    weight_ref[:, 32:, :512] = part
    weight_ref[:, 32:, 512:] = jnp.zeros((EXPERTS, 16, 128), bf16)
    sent.wait()


def attention_back_call(mine, deltas, xs, held, starts, mixture, grads):
    return pl.pallas_call(
        attention_back_kernel,
        out_shape=[
            jax.ShapeDtypeStruct((EXPERTS, 48, 640), bf16),
            jax.ShapeDtypeStruct((RING, TOK, D), bf16),
            jax.ShapeDtypeStruct(grads[0].shape, bf16),
        ],
        in_specs=[SMEM] + [HBM] * 16 + [VMEM] * 2 + [HBM] * 2,
        out_specs=[VMEM] * 2 + [HBM],
        scratch_shapes=[pltpu.VMEM((SEQ, D), bf16), pltpu.VMEM((RING, TOK, D), bf16)]
        + [pltpu.VMEM(value.shape, value.dtype) for value in held]
        + [
            pltpu.VMEM((SEQ, 256), bf16),
            pltpu.VMEM((SEQ, 256), f32),
            pltpu.VMEM((2, SEQ, 128), f32),
            pltpu.VMEM((2, SEQ, 128), f32),
            pltpu.VMEM((SEQ, 512), bf16),
            pltpu.VMEM((2,) + grads[0].shape, bf16),
            pltpu.SemaphoreType.DMA((32,)),
        ],
        compiler_params=pltpu.CompilerParams(vmem_limit_bytes=58 * MIB),
        cost_estimate=pl.CostEstimate(flops=100_000_000, bytes_accessed=100_000, transcendentals=0),
    )(mine, *deltas, *xs, *held, starts, mixture, *grads)


def unpack_kernel(own_ref, other_ref, core, query_ref, key_ref, value_ref, projection_ref, small_ref):
    first = core[0] == 0
    for half in range(2):
        rows = jnp.where(first == (half == 0), own_ref[...], other_ref[...]).astype(f32)
        span = slice(half * 128, (half + 1) * 128)
        for g in range(RING):
            query_ref[span, g * 256 : (g + 1) * 256] = rows[:, g * 512 : g * 512 + 256]
            key_ref[span, g * 128 : (g + 1) * 128] = rows[:, g * 512 + 256 : g * 512 + 384]
            value_ref[span, g * 128 : (g + 1) * 128] = rows[:, g * 512 + 384 : g * 512 + 512]
        projection_ref[span, :] = rows[:, 2048:3072]
        small_ref[span, :] = rows[:, 3072:]


def unpack_call(own, other, core):
    return pl.pallas_call(
        unpack_kernel,
        out_shape=[jax.ShapeDtypeStruct((256, width), f32) for width in (D, 512, 512, D, 128)],
        in_specs=[VMEM, VMEM, SMEM],
        out_specs=[VMEM] * 5,
        compiler_params=pltpu.CompilerParams(vmem_limit_bytes=24 * MIB),
        cost_estimate=pl.CostEstimate(flops=0, bytes_accessed=5_000_000, transcendentals=0),
    )(own, other, core)


def load_gates(copies, packs, e, gate_w, up_w):
    return [
        copies.start(packs.at[e, :, 0:256], gate_w.at[e]),
        copies.start(packs.at[e, :, 256:512], up_w.at[e]),
    ]


def load_down(copies, packs, e, down_w):
    return [
        copies.start(packs.at[e, :, 512:640], down_w.at[e, :, :, 0:512]),
        copies.start(packs.at[e, :, 640:768], down_w.at[e, :, :, 512:1024]),
    ]


def expert_kernel(groups, out_groups, order, at, *refs):
    count, out_count = len(groups), len(out_groups)
    x_refs, refs = refs[:count], refs[count:]
    (cots, info_ref, packs), refs = refs[:3], refs[3:]
    sent_refs, refs = refs[:out_count], refs[out_count:]
    (xs_ref, dy_ref, inner_ref, dg_ref, du_ref), refs = refs[:5], refs[5:]
    (x_v, c_v, info_v, gate_w, up_w, down_w, sent_v, scatter_v), refs = refs[:8], refs[8:]
    (xs_v, dy_v, inner_v, dg_v, du_v, sems) = refs
    chip = at[18]
    copies = Copies(sems)
    sources = [(g, k) for g in range(count) for k in range(groups[g])]
    targets = [(g, k) for g in range(out_count) for k in range(out_groups[g])]
    info_in = copies.start(info_ref, info_v)
    starts = [sum(groups[:g]) for g in range(count)]
    x_in = [copies.start(x_refs[g], x_v.at[pl.ds(starts[g] * TOK, groups[g] * TOK)]) for g in range(count)]
    gates_in, downs_in = [load_gates(copies, packs, 0, gate_w, up_w)], []
    c_in = [copies.start(cots.at[at[order[s]]], c_v.at[s]) for s in range(len(sources))]
    downs_in.append(load_down(copies, packs, 0, down_w))
    gates_in.append(load_gates(copies, packs, 1, gate_w, up_w))
    downs_in.append(load_down(copies, packs, 1, down_w))
    rows = 2 * CAP
    upper = lax.broadcasted_iota(jnp.int32, (rows, 256), 0) < CAP
    pick_at = lax.broadcasted_iota(jnp.int32, (rows, 256), 0)
    pick_at = jnp.where(upper, pick_at, pick_at - CAP).astype(f32)
    tall_at = lax.broadcasted_iota(jnp.int32, (TOK, rows), 1)
    scatter_at = jnp.where(tall_at < CAP, tall_at, tall_at - CAP).astype(f32)
    kind = lax.broadcasted_iota(jnp.int32, (8, rows), 0)
    expert = jnp.where(lax.broadcasted_iota(jnp.int32, (8, rows), 1) < CAP, 0, 1)
    slot_of = (kind == expert).astype(f32).astype(bf16)
    x_parts, dy_parts, picks, weighted = [], [], [], []
    for s in range(len(sources)):
        if s == 0:
            info_in.wait()
        if sources[s][1] == 0:
            x_in[sources[s][0]].wait()
        info = info_v[at[order[s]]]
        pick = jnp.where(upper, info[0:1], info[1:2]) == pick_at
        picks.append(pick.astype(f32))
        chosen = picks[s][:, :TOK].astype(bf16)
        weighted.append(jnp.where(pick, jnp.where(upper, info[2:3], info[3:4]), 0.0)[:, :TOK].astype(bf16))
        info_b = info[:, :TOK].astype(bf16)
        scatter = contract_rows(info_b, slot_of) == scatter_at
        scatter_v[s] = scatter.astype(f32).astype(bf16)
        x_parts.append(dot(chosen, x_v[s * TOK : (s + 1) * TOK, :]))
    out = []
    back, back_gate = [], []
    for e in range(2):
        span = slice(e * CAP, (e + 1) * CAP)
        xs = jnp.concatenate([part[span] for part in x_parts], axis=0).astype(bf16)
        xs_v[e] = xs
        out.append(copies.start(xs_v.at[e], xs_ref.at[e]))
        wait_all(gates_in[e])
        gate_values = dot(xs, gate_w[e].reshape(D, FF))
        up_values = dot(xs, up_w[e].reshape(D, FF))
        if e == 0:
            for s in range(len(sources)):
                c_in[s].wait()
                dy_parts.append(dot(weighted[s], c_v[s]))
        dy = jnp.concatenate([part[span] for part in dy_parts], axis=0).astype(bf16)
        dy_v[e] = dy
        out.append(copies.start(dy_v.at[e], dy_ref.at[e]))
        wait_all(downs_in[e])
        inner_delta = contract_last(dy, down_w[e].reshape(FF, D))
        sigmoid = jax.nn.sigmoid(gate_values)
        silu = gate_values * sigmoid
        inner = silu * up_values
        inner_v[e] = inner.astype(bf16)
        back_gate.append(jnp.sum(inner * inner_delta, axis=1, keepdims=True))
        dg = (inner_delta * up_values * sigmoid * (1.0 + gate_values * (1.0 - sigmoid))).astype(bf16)
        du = (inner_delta * silu).astype(bf16)
        dg_v[e] = dg
        du_v[e] = du
        for value, ref in ((inner_v, inner_ref), (dg_v, dg_ref), (du_v, du_ref)):
            out.append(copies.start(value.at[e], ref.at[e]))
        back.append(contract_last(dg, gate_w[e].reshape(D, FF)) + contract_last(du, up_w[e].reshape(D, FF)))
    row_at = lax.broadcasted_iota(jnp.int32, (16, D), 0)
    for s, (g, k) in enumerate(targets):
        span = slice(s * CAP, (s + 1) * CAP)
        part = jnp.concatenate([back[0][span], back[1][span]], axis=0).astype(bf16)
        sent_v[s, :TOK, :] = dot(scatter_v[s], part).astype(bf16)
        own = [
            jnp.sum(picks[s][e * CAP : (e + 1) * CAP] * back_gate[e][span], axis=0, keepdims=True)
            for e in range(2)
        ]
        high = [value.astype(bf16).astype(f32) for value in own]
        row = jnp.concatenate(high + [own[e] - high[e] for e in range(2)], axis=1)
        sent_v[s, TOK:, :] = jnp.where(row_at == chip, row, 0.0).astype(bf16)
        out.append(copies.start(sent_v.at[s], sent_refs[g].at[pl.ds(k * SENT, SENT)]))
    wait_all(out)


def expert_call(order, at, xs, out_groups, cots, info, packs):
    groups = tuple(x.shape[0] // TOK for x in xs)
    sources = len(order)
    slots = sources * CAP
    count = len(xs)
    kept = [
        ((2, slots, D), bf16),
        ((2, slots, D), bf16),
        ((2, slots, FF), bf16),
        ((2, slots, FF), bf16),
        ((2, slots, FF), bf16),
    ]
    shapes = [jax.ShapeDtypeStruct((g * SENT, D), bf16) for g in out_groups]
    shapes += [jax.ShapeDtypeStruct(*entry) for entry in kept]
    out = pl.pallas_call(
        lambda *refs: expert_kernel(groups, out_groups, order, *refs),
        out_shape=shapes,
        in_specs=[SMEM] + [HBM] * (count + 3),
        out_specs=[HBM] * len(shapes),
        scratch_shapes=[
            pltpu.VMEM((sources * TOK, D), bf16),
            pltpu.VMEM((sources, TOK, D), bf16),
            pltpu.VMEM((16, 8, 256), f32),
            pltpu.VMEM((2, RING, 256, FF), bf16),
            pltpu.VMEM((2, RING, 256, FF), bf16),
            pltpu.VMEM((2, RING, 128, D), bf16),
            pltpu.VMEM((sources, SENT, D), bf16),
            pltpu.VMEM((sources, TOK, 2 * CAP), bf16),
        ]
        + [pltpu.VMEM(*entry) for entry in kept]
        + [pltpu.SemaphoreType.DMA((128,))],
        compiler_params=pltpu.CompilerParams(vmem_limit_bytes=58 * MIB),
        cost_estimate=pl.CostEstimate(
            flops=2 * 2 * slots * D * FF * 16, bytes_accessed=26_000_000, transcendentals=2 * slots * FF
        ),
    )(at, *xs, cots, info, packs)
    return out[: len(out_groups)], out[len(out_groups) :]


def produce_kernel(orders, at, *refs):
    count = len(orders)
    inner_refs, (packs, _, out_ref, inner_v, down_w, out_v, sems) = refs[:count], refs[count:]
    copies = Copies(sems)
    downs_in = load_down(copies, packs, 0, down_w) + load_down(copies, packs, 1, down_w)
    ins = [copies.start(inner_refs[i], inner_v.at[:, pl.ds(8 * i * CAP, 8 * CAP)]) for i in range(count)]
    wait_all(downs_in)
    outs = []
    for i, order in enumerate(orders):
        ins[i].wait()
        rows = slice(8 * i * CAP, 8 * (i + 1) * CAP)
        produced = [dot(inner_v[e, rows, :], down_w[e].reshape(FF, D)) for e in range(2)]
        for s, source in enumerate(order):
            span = slice(s * CAP, (s + 1) * CAP)
            out_v[source] = jnp.concatenate([produced[0][span], produced[1][span]], axis=0).astype(bf16)
            outs.append(copies.start(out_v.at[source], out_ref.at[at[source]]))
    wait_all(outs)


def produce_call(orders, at, kept, packs, done):
    inners = [chunk[2] for chunk in kept]
    return pl.pallas_call(
        lambda *refs: produce_kernel(orders, *refs),
        out_shape=jax.ShapeDtypeStruct((16, 2 * CAP, D), bf16),
        in_specs=[SMEM] + [HBM] * (len(orders) + 2),
        out_specs=HBM,
        scratch_shapes=[
            pltpu.VMEM((2, 16 * CAP, FF), bf16),
            pltpu.VMEM((2, RING, 128, D), bf16),
            pltpu.VMEM((16, 2 * CAP, D), bf16),
            pltpu.SemaphoreType.DMA((64,)),
        ],
        compiler_params=pltpu.CompilerParams(vmem_limit_bytes=58 * MIB),
        cost_estimate=pl.CostEstimate(
            flops=2 * 2 * 1152 * D * FF * 3, bytes_accessed=14_000_000, transcendentals=0
        ),
    )(at, *inners, packs, done)


def combine_kernel(slot_ref, gate_ref, residual_ref, rows_ref, out_ref, rows_v, sems):
    copies = Copies(sems)
    ins = [copies.start(rows_ref.at[p], rows_v.at[p]) for p in range(16)]
    lane = lax.broadcasted_iota(jnp.int32, (TOK, 2 * CAP), 1)
    slot_at = jnp.where(lane < CAP, lane, lane - CAP).astype(f32)
    at_row = lax.broadcasted_iota(jnp.int32, (128, 2 * CAP), 0)
    at_half = jnp.where(lax.broadcasted_iota(jnp.int32, (128, 2 * CAP), 1) < CAP, 0, 1)
    both = jnp.concatenate([slot_ref[...], gate_ref[...]], axis=0)
    weights = []
    for p in range(16):
        own = (at_row == 2 * p + at_half).astype(f32).astype(bf16)
        spread = dot(both, own)
        weights.append(jnp.where(spread[:TOK] == slot_at, spread[TOK:], 0.0).astype(bf16))
    total = residual_ref[...]
    for p in range(16):
        ins[p].wait()
        total = total + dot(weights[p], rows_v[p])
    out_ref[...] = total.astype(bf16)


def combine_call(slots, gates, residual, rows):
    return pl.pallas_call(
        combine_kernel,
        out_shape=jax.ShapeDtypeStruct((TOK, D), bf16),
        in_specs=[VMEM] * 3 + [HBM],
        out_specs=VMEM,
        scratch_shapes=[pltpu.VMEM((16, 2 * CAP, D), bf16), pltpu.SemaphoreType.DMA((16,))],
        compiler_params=pltpu.CompilerParams(vmem_limit_bytes=24 * MIB),
        cost_estimate=pl.CostEstimate(flops=2_000_000_000, bytes_accessed=6_000_000, transcendentals=0),
    )(slots, gates, residual, rows)


def gradient_kernel(at, *refs):
    chunks = [refs[5 * i : 5 * i + 5] for i in range((len(refs) - 8) // 5)]
    own_ref, other_ref, xs_v, dy_v, inner_v, both_v, out_v, sems = refs[-8:]
    core = at[16]
    copies = Copies(sems)
    gate_in, down_in, start = [], [], 0
    for xs, dy, inner, dg, du in chunks:
        span = pl.ds(start, xs.shape[1])
        start += xs.shape[1]
        gate_in.append(copies.start(xs, xs_v.at[:, span]))
        gate_in.append(copies.start(dg, both_v.at[:, span, 0:FF]))
        gate_in.append(copies.start(du, both_v.at[:, span, FF : 2 * FF]))
        down_in.append(copies.start(inner, inner_v.at[:, span]))
        down_in.append(copies.start(dy, dy_v.at[:, span]))
    outs = []
    for e in range(2):
        if e == 0:
            wait_all(gate_in)
        for j in range(RING):
            part = contract_rows(xs_v[e, :, j * 256 : (j + 1) * 256], both_v[e]).astype(bf16)
            out_v[e, j, 0:256, :] = part[:, :FF]
            out_v[e, j, 256:512, :] = part[:, FF:]
        if e == 0:
            wait_all(down_in)
        for j in range(RING):
            part = contract_rows(inner_v[e, :, j * 128 : (j + 1) * 128], dy_v[e]).astype(bf16)
            out_v[e, j, 512:640, :] = part[:, :512]
            out_v[e, j, 640:768, :] = part[:, 512:]
    outs.append(copies.start(out_v.at[1 - core], other_ref))
    outs.append(copies.start(out_v.at[core], own_ref))
    wait_all(outs)


def gradient_call(at, kept):
    size = sum(chunk[0].shape[1] for chunk in kept)
    operands = [entry for chunk in kept for entry in chunk]
    return pl.pallas_call(
        gradient_kernel,
        out_shape=[jax.ShapeDtypeStruct((RING, 768, 512), bf16)] * 2,
        in_specs=[SMEM] + [HBM] * len(operands),
        out_specs=[HBM] * 2,
        scratch_shapes=[
            pltpu.VMEM((2, size, D), bf16),
            pltpu.VMEM((2, size, D), bf16),
            pltpu.VMEM((2, size, FF), bf16),
            pltpu.VMEM((2, size, 2 * FF), bf16),
            pltpu.VMEM((2, RING, 768, 512), bf16),
            pltpu.SemaphoreType.DMA((64,)),
        ],
        compiler_params=pltpu.CompilerParams(vmem_limit_bytes=58 * MIB),
        cost_estimate=pl.CostEstimate(
            flops=2 * 2 * 1152 * D * FF * 6, bytes_accessed=24_000_000, transcendentals=0
        ),
    )(at, *operands)


def gather_plane(own, info):
    near = [send_plane(own, 0, d) for d in (1, 2, 3)]
    own_one, own_three = send_plane(own, 1, 1), send_plane(own, 1, 3)
    rest = jnp.concatenate(near, axis=0)
    rest_one, rest_three = send_plane(rest, 1, 1), send_plane(rest, 1, 3)
    own_two = send_plane(own_one, 1, 1)
    held = 0 * info[0, 0, 0].astype(bf16)
    low_two = send_plane(rest_one[:TOK] + held, 1, 1)
    high_two = send_plane(rest_three[TOK:] + held, 1, 3)
    return [own] + near, [own_one, rest_one], [own_two, low_two, high_two], [own_three, rest_three]


def add(left, right):
    return (left.astype(f32) + right.astype(f32)).astype(bf16)


def scatter_far(one, two, three):
    low = send_plane(two[0], 1, 3)
    high = send_plane(two[1], 1, 1)
    rest_three = jnp.concatenate([three[1][:SENT], add(three[1][SENT:], high)], axis=0)
    rest_one = jnp.concatenate([add(one[1][:SENT], low[SENT:]), one[1][SENT:]], axis=0)
    return add(one[0], low[:SENT]), rest_one, three[0], rest_three


def scatter_near(own, parts, before):
    before = 0 * before[0, 0, 0].astype(f32)
    own_one, rest_one = (send_plane(part, 1, 3) for part in parts[:2])
    own_three, rest_three = (send_plane(part, 1, 1) for part in parts[2:])
    total = own[0].astype(f32) + own_one.astype(f32) + own_three.astype(f32)
    for d in (1, 2, 3):
        span = slice((d - 1) * SENT, d * SENT)
        part = own[d].astype(f32) + before + rest_one[span].astype(f32) + rest_three[span].astype(f32)
        total = total + send_plane(part.astype(bf16), 0, -d).astype(f32)
    return total, rest_one


def sum_plane(blocks, core, along, across):
    blocks = blocks.reshape((2, RING, RING) + blocks.shape[1:])
    blocks = add(pick(blocks, core), send_core(pick(blocks, 1 - core)))
    for line, position in ((0, along), (1, across)):
        parts = [pick(blocks, position)]
        parts += [send_plane(pick(blocks, (position + d) % RING), line, d) for d in (1, 2, 3)]
        total = sum(part.astype(f32) for part in parts)
        blocks = total.astype(bf16)
    return total


def spread_plane(block, along, across, done):
    for line, position in ((1, across), (0, along)):
        block = in_order([block] + [send_plane(block, line, d) for d in (1, 2, 3)], position)
    block = block.reshape(128, block.shape[-1]) + 0 * done
    return block, send_core(block)


def body(
    hidden,
    segments,
    routes,
    attention_gain,
    query_weight,
    key_weight,
    value_weight,
    projection_weight,
    mixture_gain,
    router_weight,
    gate_weight,
    up_weight,
    down_weight,
    cotangent,
):
    me = lax.axis_index("expert")
    mine = lax.axis_index("fsdp")
    core = me % 2
    chip = me // 2
    place_z, place_x = chip // RING, chip % RING
    along = jnp.where(core == 0, place_x, place_z)
    across = jnp.where(core == 0, place_z, place_x)
    same_core = [[2 * i + c for i in range(EXPERTS // 2)] for c in range(2)]

    steps = jnp.arange(16, dtype=jnp.int32)
    from_across, from_along = (across - steps // RING) % RING, (along - steps % RING) % RING
    source_chip = jnp.where(core == 0, from_across * RING + from_along, from_along * RING + from_across)
    at = jnp.concatenate([source_chip, jnp.stack([core, mine, chip])]).astype(jnp.int32)
    here = mine.reshape(1).astype(jnp.int32)

    counts = jnp.stack([jnp.sum(segments < 1), jnp.sum(segments < 2)]).astype(bf16)
    notes = jnp.stack([jnp.concatenate([attention_gain, mixture_gain]), jnp.pad(counts, (0, 510))])
    notes = jnp.pad(notes, ((0, 6), (0, 512)))
    notes = jnp.concatenate([notes, router_weight.T.reshape(4, 8, 256).transpose(1, 0, 2).reshape(8, D)], axis=0)
    head_weights = jnp.concatenate(
        [w.reshape(256, RING, -1) for w in (query_weight, key_weight, value_weight)], axis=2
    ).transpose(1, 0, 2)
    head_weights = jnp.concatenate([head_weights[:, :128], head_weights[:, 128:]], axis=2)

    def message(d):
        return jnp.concatenate([hidden, pick(head_weights, (mine + d) % RING), notes], axis=0)

    messages = [message(0)] + [send_y(message(d), d) for d in (1, 2, 3)]

    named = (routes[:, :, None] == jnp.arange(EXPERTS, dtype=jnp.int32)[None, None, :]).astype(f32).sum(axis=1)
    lower = (jnp.arange(TOK)[:, None] > jnp.arange(TOK)[None, :]).astype(bf16)
    rank = dot(lower, named.astype(bf16))
    slot = jnp.where(named > 0, rank, -1000.0)
    cots = lax.all_gather(cotangent, "expert", axis_index_groups=same_core)

    cosines, sines = rotary_table()
    act, qkv, mixed_heads, mixed_parts, own_w, starts, router = attention_call(
        here, messages, cosines, sines, projection_weight
    )

    mixed_parts = [mixed_parts[0]] + [send_y(mixed_parts[r], -r) for r in (1, 2, 3)]

    gain_two = in_order([part[320:321, 256:512] for part in messages], mine).reshape(D).astype(f32)


    residual = hidden.astype(f32)
    residual_two = residual + sum(part.astype(f32) for part in mixed_parts)
    scale_two = scale_of(residual_two)
    expert_input = (residual_two * scale_two * gain_two).astype(bf16)

    down_halves = jnp.concatenate([down_weight[0][:, :512], down_weight[0][:, 512:]], axis=0)
    pack = jnp.concatenate([gate_weight[0], up_weight[0], down_halves], axis=0)
    pack = pack + 0 * scale_two[0, 0].astype(bf16)
    chip_groups = [[(2 * i + c) * RING + y for c in range(2) for y in range(RING)] for i in range(EXPERTS // 2)]
    packs = lax.all_gather(pack, ("expert", "fsdp"), axis_index_groups=chip_groups).reshape(2, RING, 768, 512)

    logits = contract_last(expert_input, router)[:, :EXPERTS]
    logits = jnp.where(named > 0, logits, -1e30)
    gate_weights = jnp.where(named > 0, jnp.exp(logits - jnp.max(logits, axis=1, keepdims=True)), 0.0)
    gate_weights = gate_weights / jnp.sum(gate_weights, axis=1, keepdims=True)
    info = jnp.stack([slot, gate_weights + 0 * cots[0, 0, 0].astype(f32)]).transpose(2, 0, 1).reshape(16, 2, 2, TOK).transpose(0, 2, 1, 3)
    info = jnp.pad(info.reshape(16, 4, TOK), ((0, 0), (0, 4), (0, 256 - TOK)), constant_values=-1000.0)
    info = lax.all_to_all(info, "expert", 0, 0, axis_index_groups=same_core, tiled=True)

    x_blocks = gather_plane(expert_input, info)
    orders = [[4, 5, 6, 7, 12, 13, 14, 15], [8, 9, 10, 11, 0, 1, 2, 3]]
    arrivals = [x_blocks[1] + x_blocks[3], x_blocks[2] + x_blocks[0]]
    layouts = [(1, 3, 1, 3), (2, 2, 1, 1, 1, 1)]
    sent, kept = zip(
        *[
            expert_call(orders[i], at, arrivals[i], layouts[i], cots, info, packs)
            for i in range(2)
        ]
    )
    near_parts = scatter_far(sent[0][:2], sent[1][:2], sent[0][2:])
    own_grad, other_grad = gradient_call(at, kept)
    returned, arrived = scatter_near(sent[1][2:], near_parts, own_grad)
    route_delta = returned[:TOK]
    gate_back = returned[TOK:, :512] + returned[TOK:, 512:]
    gate_back = gate_back.reshape(16, 2, 256)[:, :, :TOK].reshape(EXPERTS, TOK).T

    logit_delta = (gate_back - gate_weights * jnp.sum(gate_back, axis=1, keepdims=True)).astype(bf16)
    router_part = contract_rows(expert_input, jnp.pad(logit_delta, ((0, 0), (0, 96))))
    input_delta = route_delta + dot(logit_delta, router[:EXPERTS])
    mixture_part = jnp.sum(input_delta * residual_two * scale_two, axis=0)
    inner = input_delta * gain_two
    upstream = cotangent.astype(f32)
    residual_delta = upstream + scale_two * (
        inner - residual_two * scale_two * scale_two * jnp.mean(inner * residual_two, axis=-1, keepdims=True)
    )
    attention_delta = residual_delta.astype(bf16)

    attention_deltas = [attention_delta] + [send_y(attention_delta, d) for d in (1, 2, 3)]
    weight_part, activation_part, total_grad = attention_back_call(
        here,
        attention_deltas,
        messages,
        [projection_weight, qkv, cosines, sines, mixed_heads, router_part, act, own_w],
        starts,
        mixture_part[None],
        [own_grad, send_core(other_grad)],
    )
    expert_total = lax.psum_scatter(total_grad.reshape(RING * 768, 512), "fsdp", tiled=True)

    produced = produce_call(orders, at, kept, packs, arrived)
    produced = lax.all_to_all(produced, "expert", 0, 0, axis_index_groups=same_core, tiled=True)
    wide = ((0, 0), (0, 128 - EXPERTS))
    output = combine_call(
        jnp.pad(slot, wide, constant_values=-1000.0).astype(bf16),
        jnp.pad(gate_weights, wide).astype(bf16),
        residual_two,
        produced,
    )

    activation_parts = [activation_part[0]] + [send_y(activation_part[r], -r) for r in (1, 2, 3)]
    activation_delta = sum(part.astype(f32) for part in activation_parts)
    scale_one = scale_of(residual)
    gain_one = in_order([part[320:321, :256] for part in messages], mine).reshape(D).astype(f32)
    inner = activation_delta * gain_one
    input_gradient = residual_delta + scale_one * (
        inner - residual * scale_one * scale_one * jnp.mean(inner * residual, axis=-1, keepdims=True)
    )

    shared = sum_plane(weight_part, core, along, across)
    held = 0 * (activation_delta[0, 0] + produced[0, 0, 0].astype(f32))
    pieces = (shared[:32].reshape(RING, 8, 640) + held).astype(bf16)
    received = [pick(pieces, mine)] + [send_y(pick(pieces, (mine + d) % RING), d) for d in (1, 2, 3)]
    small = sum(part[:, 512:].astype(f32) for part in received) + 0 * output[0, 0].astype(f32)
    late = in_order([part[:, :512] for part in received], mine)
    shared = jnp.concatenate([late[g] for g in range(RING)] + [shared[32:40, :512], shared[40:, :512], small], axis=1)
    own, other = spread_plane(shared.astype(bf16), along, across, expert_total[0, 0])
    query_gradient, key_gradient, value_gradient, projection_gradient, small = unpack_call(
        own, other, core.reshape(1).astype(jnp.int32)
    )

    expert_total = expert_total.astype(f32)
    gate_gradient = expert_total[None, :256]
    up_gradient = expert_total[None, 256:512]
    down_gradient = jnp.concatenate([expert_total[512:640], expert_total[640:]], axis=1)[None]

    return (
        output,
        input_gradient,
        small[:, 33],
        query_gradient,
        key_gradient,
        value_gradient,
        projection_gradient,
        small[:, 32],
        small[:, :32],
        gate_gradient,
        up_gradient,
        down_gradient,
    )


def solution(mesh):
    rows = P(("expert", "fsdp"), None)
    weights = P("fsdp", None)
    experts = P("expert", "fsdp", None)
    return jax.shard_map(
        body,
        mesh=mesh,
        in_specs=(
            rows,
            P(("expert", "fsdp")),
            rows,
            P("fsdp"),
            weights,
            weights,
            weights,
            weights,
            P("fsdp"),
            weights,
            experts,
            experts,
            experts,
            rows,
        ),
        out_specs=(
            rows,
            rows,
            P("fsdp"),
            weights,
            weights,
            weights,
            weights,
            P("fsdp"),
            weights,
            experts,
            experts,
            experts,
        ),
        check_vma=False,
    )
```
